256 devices in a mesh: layer: 8 (over z_lo, y), feat: 32 (over z_hi, x, core).
Axes of the slice: x: 4, y: 4, z: 8 (z_hi: 4, z_lo: 2; z = z_hi * 2 + z_lo), core: 2. Of those that a mesh axis runs over, the one named last changes fastest.
Arguments:
- source: bfloat16 [512, 4096], P(None, 'layer'), may hold values from -6 to 6
- enc_weight: bfloat16 [4096, 16384], P('layer', 'feat'), may hold values from -0.09375 to 0.09375
- enc_bias: float32 [16384], P('feat'), may hold values from -0.5 to 0.5
- dec_weight: bfloat16 [8, 16384, 4096], P('layer', 'feat'), may hold values from -0.046875 to 0.046875
- dec_bias: float32 [8, 4096], P('layer'), may hold values from -3 to 3
- target: bfloat16 [8, 512, 4096], P('layer'), may hold values from -36 to 36
Outputs:
- grad_enc: float32 [4096, 16384], P('layer', 'feat')
- grad_enc_bias: float32 [16384], P('feat')
- grad_dec: bfloat16 [8, 16384, 4096], P('layer', 'feat')
- grad_dec_bias: float32 [8, 4096], P('layer', 'feat')
- loss: float32 [], replicated
The draws below stay inside these ranges and needn't reach their ends.
All inputs are finite; a program needn't handle non-finite values.
Results may differ from the reference program's by a relative error of at most 0.0049.
Values may be sent and summed in bfloat16 or wider, within the bound.
A program may use at most 128 MiB of HBM per device.

```python
import jax
import jax.numpy as jnp
from jax import lax

D = 4096
F = 16384
TOKENS = 512
L = 8


def draw_target(key, part):
    key = jax.random.fold_in(key, 11)
    first = jax.random.fold_in(key, 0)
    third = jax.random.fold_in(key, 2)
    depth = jnp.arange(L, dtype=jnp.float32) / (L - 1)
    column = jnp.arange(D, dtype=jnp.float32) / (D - 1)
    rough = jnp.exp(jax.random.uniform(third, (1, 1, D), jnp.float32, -0.5, 0.5))
    scale = (1.0 + 2.0 * depth)[:, None, None] * ((1.0 + 2.0 * column)[None, None, :] * rough)
    base = jnp.clip(jax.random.normal(first, (L, TOKENS, D), jnp.float32), -4.0, 4.0)
    return (base * scale * 0.6).astype(jnp.bfloat16)


def levels(own_key, dims, cuts, least, largest):
    def one(dim, parts):
        draws = jax.random.uniform(jax.random.fold_in(jax.random.fold_in(own_key, 6), dim), (parts,), jnp.float32, least / len(cuts), largest / len(cuts))
        return jnp.repeat(jnp.exp(draws), dims[dim] // parts).reshape((-1,) + (1,) * (len(dims) - dim - 1))

    factor_of = one(*cuts[0])
    for cut in cuts[1:]:
        factor_of = factor_of * one(*cut)
    return factor_of


def gaussian(own_key, dims, width, limit, cuts=(), kind=jnp.bfloat16):
    gain = levels(own_key, dims, cuts, -0.22, 0.18) if cuts else 1.0
    result = jax.random.normal(own_key, dims, jnp.float32) * width * gain
    return jnp.minimum(jnp.maximum(result, -limit), limit).astype(kind)


def setup_inputs(seed: int = 0) -> dict:
    arg_keys = jax.random.split(jax.random.key(seed), 7)
    return {
        "source": gaussian(arg_keys[0], (TOKENS, D), 1.0, 6.0, ((1, 8),)),
        "enc_weight": gaussian(arg_keys[1], (D, F), D ** -0.5, 0.09375, ((0, 8), (1, 32))),
        "enc_bias": jnp.clip(jax.random.uniform(arg_keys[2], (F,), jnp.float32, -0.5, 0.5) * levels(arg_keys[2], (F,), ((0, 32),), -0.4, 0.0), -0.5, 0.5),
        "dec_weight": gaussian(arg_keys[3], (L, F, D), F ** -0.5, 0.046875, ((0, 8), (1, 32))),
        "dec_bias": gaussian(arg_keys[4], (L, D), 0.5, 3.0, ((0, 8),), jnp.float32),
        "target": draw_target(jax.random.fold_in(arg_keys[6], 71), 0),
    }


def activate(pre):
    return jax.nn.gelu(pre, approximate=True)

def reference(source, enc_weight, enc_bias, dec_weight, dec_bias, target):
    pre = jnp.dot(source, enc_weight, preferred_element_type=jnp.float32) + enc_bias
    acts = activate(pre).astype(jnp.bfloat16)

    def one_layer(carry, items):
        weight, bias, goal = items
        err = jnp.dot(acts, weight, preferred_element_type=jnp.float32) + bias - goal.astype(jnp.float32)
        err_b = err.astype(jnp.bfloat16)
        grad_w = lax.dot_general(acts, err_b, (((0,), (0,)), ((), ())), preferred_element_type=jnp.float32).astype(jnp.bfloat16)
        back = lax.dot_general(err_b, weight, (((1,), (1,)), ((), ())), preferred_element_type=jnp.float32)
        total, squares = carry
        return ((total + back, squares + jnp.sum(err * err)), (grad_w, lax.optimization_barrier(jnp.sum(err, axis=0))))
    start = (jnp.zeros(pre.shape, jnp.float32), jnp.zeros((), jnp.float32))
    (back, squares), (grad_dec, grad_dec_bias) = lax.scan(one_layer, start, (dec_weight, dec_bias, target))
    _, pullback = jax.vjp(activate, pre)
    dpre = pullback(back)[0]
    grad_enc_bias = lax.optimization_barrier(jnp.sum(dpre, axis=0))
    grad_enc = lax.dot_general(source, dpre.astype(jnp.bfloat16), (((0,), (0,)), ((), ())), preferred_element_type=jnp.float32)
    loss = squares / (2.0 * TOKENS * L * D)
    return (grad_enc, grad_enc_bias, grad_dec, grad_dec_bias, loss)
```

```python
import functools

import jax
import jax.numpy as jnp
from jax import lax
from jax.experimental import pallas as pl
from jax.experimental.pallas import tpu as pltpu
from jax.sharding import PartitionSpec as P

BF = jnp.bfloat16
F32 = jnp.float32
MESH = pl.DeviceIdType.MESH

NY, NX, NZ = 4, 4, 4
CHUNK = 64
LAG = dict(P1=0, P2=1, P3=2, P4=3, P5=4, P6A=5, P6=6, P7=7, P8=8, P8A=9, P9=10, P10=11, P11=12, P12=13, P13=14)
ORDER = ("P13", "P12", "P11", "P10", "P9", "P8A", "P8", "P7", "P6", "P6A", "P5", "P4", "P3", "P2", "P1")
KINDS = ("YR", "ZP", "YA", "SA", "HP", "HM", "OP", "OM", "AP", "AM", "ZR", "ZA", "XP", "XM", "FP", "FM", "SB", "YB", "ZB", "YD")
ID = {name: i for i, name in enumerate(KINDS)}
ONCE = ("W", "GB", "L1", "L2", "L3", "L4", "L5", "GD")
OID = {name: i for i, name in enumerate(ONCE)}
A0 = 0.7978845608
A1 = 0.044715


def dot(a, b, dims):
    return lax.dot_general(a, b, (dims, ((), ())), preferred_element_type=F32)


def kernel(
    src_h, enc_h, encb_v, w_h, decb_v, tgt_h,
    ge_v, geb_v, gd_h, gdb_v, loss_s,
    src, enc, tgt, w, ps, ry, zs_p, zr_p, gpr, acts, rec, own, hp, hm, op, om, ap, am, sp, sm, zsend, zown, rz, eall,
    b_own, b_send, b_recv, by, ryb, zs_b, zr_b, dall, gd, pb, rpb, sq, rl1, rl2, rl3, rl4, rl5, sl2, sl3, sl4, sl5, bsum,
    lsem, ssem, rsem, oss, ors,
):
    tok, depth = src.shape
    feats = enc.shape[1]
    half = w.shape[1]
    tt = CHUNK
    nch = tok // tt
    rows = tt // NY
    group = half // NX
    hg = group // 2
    blk = group // NZ
    lay, fea = lax.axis_index("layer"), lax.axis_index("feat")
    zl, y = lay // NY, lay % NY
    zh, x, core = fea // (2 * NX), (fea // 2) % NX, fea % 2

    def dev(dzl=0, dy=0, dzh=0, dx=0, dc=0):
        return (
            ((zl + dzl) % 2) * NY + (y + dy) % NY,
            ((zh + dzh) % NZ) * (2 * NX) + ((x + dx) % NX) * 2 + (core + dc) % 2,
        )

    def send(kind, k, src_ref, dst_ref, to):
        pltpu.make_async_remote_copy(
            src_ref, dst_ref, ssem.at[ID[kind]], rsem.at[ID[kind], k], device_id=to, device_id_type=MESH
        ).start()

    def got(kind, k, ref):
        pltpu.make_async_copy(ref, ref, rsem.at[ID[kind], k]).wait()

    def send1(kind, src_ref, dst_ref, to):
        pltpu.make_async_remote_copy(
            src_ref, dst_ref, oss.at[OID[kind]], ors.at[OID[kind]], device_id=to, device_id_type=MESH
        ).start()

    def got1(kind, ref):
        pltpu.make_async_copy(ref, ref, ors.at[OID[kind]]).wait()

    barrier = pltpu.get_barrier_semaphore()
    peers = (
        [dict(dy=o) for o in range(1, NY)] + [dict(dzl=1), dict(dc=1)]
        + [dict(dx=o) for o in range(1, NX)] + [dict(dzh=o) for o in range(1, NZ)]
    )
    for p in peers:
        pl.semaphore_signal(barrier, inc=1, device_id=dev(**p), device_id_type=MESH)

    c_src = pltpu.make_async_copy(src_h, src, lsem.at[0])
    c_enc = pltpu.make_async_copy(enc_h, enc, lsem.at[1])
    c_src.start()
    c_enc.start()

    def column(o, p, c):
        return pl.multiple_of((((zh + p) % NZ) * (2 * NX) + ((x + o) % NX) * 2 + c) * blk, blk)

    for o in range(NX):
        for p in range(NZ):
            pltpu.make_async_copy(
                w_h.at[0, :, pl.ds(column(o, p, core), blk)],
                w.at[pl.ds(0, feats), pl.ds((o * NZ + p) * blk, blk)],
                lsem.at[2],
            ).start()
    c_tgt = pltpu.make_async_copy(tgt_h.at[0, :, pl.ds(pl.multiple_of(fea * blk, blk), blk)], tgt, lsem.at[3])
    c_tgt.start()
    pl.semaphore_wait(barrier, len(peers))
    for o in range(NX):
        for p in range(NZ):
            send1(
                "W", w_h.at[0, :, pl.ds(column(o, p, 1 - core), blk)],
                w.at[pl.ds(feats, feats), pl.ds((o * NZ + p) * blk, blk)], dev(dc=1),
            )
    sq[...] = jnp.zeros_like(sq)
    pb[...] = jnp.zeros_like(pb)
    bsum[...] = jnp.zeros_like(bsum)
    c_src.wait()
    c_enc.wait()

    def span(k):
        return pl.ds(pl.multiple_of(k * tt, tt), tt)

    def piece(k, yy):
        return pl.ds(pl.multiple_of(k * tt + yy * rows, rows), rows)

    def fold(v):
        return jnp.sum(v.reshape(v.shape[0] // 8, 8, v.shape[1]), axis=0)

    def p1(k):
        ps[span(k)] = dot(src[span(k)], enc[...], ((1,), (0,)))
        for o in range(1, NY):
            send("YR", k, ps.at[piece(k, (y + o) % NY)], ry.at[k, o - 1], dev(dy=o))

    def p2(k):
        got("YR", k, ry.at[k])
        zs_p[k] = ps[piece(k, y)] + ry[k, 0] + ry[k, 1] + ry[k, 2]
        send("ZP", k, zs_p.at[k], zr_p.at[k], dev(dzl=1))

    def p3(k):
        got("ZP", k, zr_p.at[k])
        v = zs_p[k] + zr_p[k] + encb_v[...]
        v2 = v * v
        t = jnp.tanh(A0 * (v * (1.0 + A1 * v2)))
        h = 0.5 * (1.0 + t)
        acts[piece(k, y), pl.ds(0, feats)] = (v * h).astype(BF)
        for o in range(1, NY):
            r = acts.at[piece(k, y), pl.ds(0, feats)]
            send("YA", k, r, r, dev(dy=o))
        gpr[k] = h + 0.5 * v * (1.0 - t * t) * (A0 * (1.0 + 3.0 * A1 * v2))

    def p4(k):
        got("YA", k, acts.at[pl.ds(0, 3 * rows), pl.ds(0, feats)])
        send("SA", k, acts.at[span(k), pl.ds(0, feats)], acts.at[span(k), pl.ds(feats, feats)], dev(dc=1))

    def p5(k):
        got("SA", k, acts.at[span(k), pl.ds(feats, feats)])

        @pl.when(k == 0)
        def _():
            pltpu.make_async_copy(w.at[pl.ds(0, feats)], w.at[pl.ds(0, feats)], lsem.at[2]).wait()
            got1("W", w.at[pl.ds(feats, feats)])

        a = acts[span(k)]
        s = span(k)
        for o in (2, 1, 3):
            rec[s, pl.ds(o * group, group)] = dot(a, w[:, pl.ds(o * group, group)], ((1,), (0,))).astype(BF)
            if o == 2:
                send("HP", k, rec.at[s, pl.ds(2 * group, hg)], hp.at[s], dev(dx=1))
                send("HM", k, rec.at[s, pl.ds(2 * group + hg, hg)], hm.at[s], dev(dx=3))
            elif o == 1:
                send("OP", k, rec.at[s, pl.ds(group + hg, hg)], op.at[s], dev(dx=1))
            else:
                send("OM", k, rec.at[s, pl.ds(3 * group, hg)], om.at[s], dev(dx=3))
        own[s] = dot(a, w[:, pl.ds(0, group)], ((1,), (0,)))

    def p6a(k):
        s = span(k)
        got("HP", k, hp.at[s])
        sp[s] = (hp[s].astype(F32) + rec[s, pl.ds(group, hg)].astype(F32)).astype(BF)
        send("AP", k, sp.at[s], ap.at[s], dev(dx=1))
        got("HM", k, hm.at[s])
        sm[s] = (hm[s].astype(F32) + rec[s, pl.ds(3 * group + hg, hg)].astype(F32)).astype(BF)
        send("AM", k, sm.at[s], am.at[s], dev(dx=3))

    def p6(k):
        s = span(k)
        got("OP", k, op.at[s])
        got("OM", k, om.at[s])
        got("AP", k, ap.at[s])
        got("AM", k, am.at[s])
        first = own[s, pl.ds(0, hg)] + ap[s].astype(F32) + om[s].astype(F32)
        second = own[s, pl.ds(hg, hg)] + am[s].astype(F32) + op[s].astype(F32)
        zown[s] = first[:, :blk]
        zsend[s, pl.ds(0, hg)] = first.astype(BF)
        zsend[s, pl.ds(hg, hg)] = second.astype(BF)
        for p in range(1, NZ):
            send("ZR", k, zsend.at[s, pl.ds(p * blk, blk)], rz.at[k, p - 1], dev(dzh=p))

    def p7(k):
        s = span(k)
        got("ZR", k, rz.at[k])
        recon = zown[s] + rz[k, 0].astype(F32) + rz[k, 1].astype(F32) + rz[k, 2].astype(F32)

        @pl.when(k == 0)
        def _():
            c_tgt.wait()

        err = recon + decb_v[:, pl.ds(pl.multiple_of(fea * blk, blk), blk)] - tgt[s].astype(F32)
        eall[s, pl.ds(0, blk)] = err.astype(BF)
        for p in range(1, NZ):
            send("ZA", k, eall.at[s, pl.ds(0, blk)], eall.at[s, pl.ds((NZ - p) * blk, blk)], dev(dzh=p))
        bsum[...] += fold(err)
        sq[...] += fold(err * err)

    def p8(k):
        s = span(k)
        got("ZA", k, eall.at[s, pl.ds(blk, 3 * blk)])
        send("XP", k, eall.at[s, pl.ds(0, group)], eall.at[s, pl.ds(3 * group, group)], dev(dx=1))
        send("XM", k, eall.at[s, pl.ds(0, group)], eall.at[s, pl.ds(group, group)], dev(dx=3))

    def p8a(k):
        s = span(k)
        got("XP", k, eall.at[s, pl.ds(3 * group, group)])
        send("FP", k, eall.at[s, pl.ds(3 * group, hg)], eall.at[s, pl.ds(2 * group, hg)], dev(dx=1))
        got("XM", k, eall.at[s, pl.ds(group, group)])
        send("FM", k, eall.at[s, pl.ds(group + hg, hg)], eall.at[s, pl.ds(2 * group + hg, hg)], dev(dx=3))

    def p9(k):
        s = span(k)
        got("FP", k, eall.at[s, pl.ds(2 * group, hg)])
        got("FM", k, eall.at[s, pl.ds(2 * group + hg, hg)])
        e = eall[s]
        b_send[s] = dot(e, w[pl.ds(feats, feats)], ((1,), (1,)))
        send("SB", k, b_send.at[s], b_recv.at[s], dev(dc=1))
        b_own[s] = dot(e, w[pl.ds(0, feats)], ((1,), (1,)))

    def p10(k):
        s = span(k)
        got("SB", k, b_recv.at[s])
        by[s] = (b_own[s] + b_recv[s]).astype(BF)
        for o in range(1, NY):
            send("YB", k, by.at[piece(k, (y + o) % NY)], ryb.at[k, o - 1], dev(dy=o))

    def p11(k):
        got("YB", k, ryb.at[k])
        me = piece(k, y)
        zs_b[k] = (
            b_own[me] + b_recv[me] + ryb[k, 0].astype(F32) + ryb[k, 1].astype(F32) + ryb[k, 2].astype(F32)
        )
        send("ZB", k, zs_b.at[k], zr_b.at[k], dev(dzl=1))

    def p12(k):
        got("ZB", k, zr_b.at[k])
        dpre = (zs_b[k] + zr_b[k]) * gpr[k]
        r = dall.at[piece(k, y)]
        dall[piece(k, y)] = dpre.astype(BF)
        for o in range(1, NY):
            send("YD", k, r, r, dev(dy=o))
        pb[...] += fold(dpre)

        @pl.when(k == nch - 1)
        def _():
            for o in range(1, NY):
                send1("GB", pb, rpb.at[o - 1], dev(dy=o))

    def p13(k):
        got("YD", k, dall.at[pl.ds(0, 3 * rows)])

    stages = dict(P1=p1, P2=p2, P3=p3, P4=p4, P5=p5, P6A=p6a, P6=p6, P7=p7, P8=p8, P8A=p8a, P9=p9, P10=p10, P11=p11, P12=p12, P13=p13)

    def grad(base, which):
        def body(n, _):
            at = pl.multiple_of(n * group, group)
            gd[pl.ds(base, feats), pl.ds(at, group)] = dot(
                acts[:, pl.ds(base, feats)], eall[:, pl.ds(at, group)], ((0,), (0,))
            ).astype(BF)
            for p in range(NZ):
                part = gd.at[pl.ds(base, feats), pl.ds(pl.multiple_of(at + p * blk, blk), blk)]
                where = gd_h.at[0, :, pl.ds(column(n, p, core), blk)]
                if which:
                    send1("GD", part, where, dev(dc=1))
                else:
                    pltpu.make_async_copy(part, where, lsem.at[4]).start()
            return 0

        lax.fori_loop(0, NX, body, 0)

    def l1():
        for o in range(1, NZ):
            send1("L1", sq, rl1.at[o - 1], dev(dzh=o))

    def l2():
        got1("L1", rl1)
        sl2[...] = sq[...] + rl1[0] + rl1[1] + rl1[2]
        for o in range(1, NX):
            send1("L2", sl2, rl2.at[o - 1], dev(dx=o))

    def l3():
        got1("L2", rl2)
        sl3[...] = sl2[...] + rl2[0] + rl2[1] + rl2[2]
        send1("L3", sl3, rl3, dev(dc=1))

    def l4():
        got1("L3", rl3)
        sl4[...] = sl3[...] + rl3[...]
        for o in range(1, NY):
            send1("L4", sl4, rl4.at[o - 1], dev(dy=o))

    def l5():
        got1("L4", rl4)
        sl5[...] = sl4[...] + rl4[0] + rl4[1] + rl4[2]
        send1("L5", sl5, rl5, dev(dzl=1))

    last = nch - 1
    extra = {
        "P7": [(LAG["P7"] + last, l1)],
        "P8": [(LAG["P8"] + last, l2)],
        "P8A": [(LAG["P8A"] + last, l3)],
        "P10": [(LAG["P10"] + last, lambda: grad(feats, True)), (LAG["P10"] + last, l4)],
        "P11": [(LAG["P11"] + last, lambda: grad(0, False)), (LAG["P11"] + last, l5)],
    }

    def iteration(t, _):
        for name in ORDER:
            k = t - LAG[name]

            @pl.when((k >= 0) & (k < nch))
            def _(name=name, k=k):
                stages[name](k)

            for when, what in extra.get(name, ()):
                pl.when(t == when)(what)
        return 0

    lax.fori_loop(0, max(LAG.values()) + nch, iteration, 0)

    ge_v[...] = dot(src[...], dall[...], ((0,), (0,)))
    got1("GB", rpb)
    geb_v[...] = jnp.sum(pb[...] + rpb[0] + rpb[1] + rpb[2], axis=0, keepdims=True)
    gdb_v[...] = jnp.sum(bsum[...], axis=0, keepdims=True)
    got1("L5", rl5)
    layers = 2 * NY
    width = 2 * half
    loss_s[0, 0] = jnp.sum(sl5[...] + rl5[...]) / (2.0 * tok * layers * width)

    own_gd = gd.at[pl.ds(0, feats)]
    pltpu.make_async_copy(own_gd, own_gd, lsem.at[4]).wait()
    got1("GD", own_gd)
    q3 = 3 * tok // 4
    left = dict(
        YR=ry, ZP=zr_p, YA=acts.at[pl.ds(0, q3), pl.ds(0, feats)], SA=acts.at[:, pl.ds(0, feats)], HP=hp, HM=hm, OP=op, OM=om,
        AP=ap, AM=am, ZR=rz, ZA=eall.at[:, pl.ds(0, 3 * blk)], XP=eall.at[:, pl.ds(0, group)], XM=eall.at[:, pl.ds(0, group)],
        FP=hp, FM=hm, SB=b_recv, YB=ryb, ZB=zr_b, YD=dall.at[pl.ds(0, q3)],
    )
    for name, ref in left.items():
        pltpu.make_async_copy(ref, ref, ssem.at[ID[name]]).wait()
    once = dict(W=w.at[pl.ds(0, feats)], GB=rpb, L1=rl1, L2=rl2, L3=rl3, L4=rl4, L5=rl5, GD=own_gd)
    for name, ref in once.items():
        pltpu.make_async_copy(ref, ref, oss.at[OID[name]]).wait()


def shards(source, enc_weight, enc_bias, dec_weight, dec_bias, target):
    tok, depth = source.shape
    feats = enc_weight.shape[1]
    width = dec_weight.shape[2]
    half = width // 2
    group = half // NX
    hg = group // 2
    blk = group // NZ
    nch = tok // CHUNK
    rows = CHUNK // NY
    V = pltpu.VMEM
    any_spec = pl.BlockSpec(memory_space=pl.ANY)
    vmem_spec = pl.BlockSpec(memory_space=pltpu.VMEM)
    scratch = [
        V((tok, depth), BF), V((depth, feats), BF), V((tok, blk), BF), V((2 * feats, half), BF),
        V((tok, feats), F32), V((nch, 3, rows, feats), F32), V((nch, rows, feats), F32), V((nch, rows, feats), F32),
        V((nch, rows, feats), F32), V((tok, 2 * feats), BF), V((tok, half), BF), V((tok, group), F32),
        V((tok, hg), BF), V((tok, hg), BF), V((tok, hg), BF), V((tok, hg), BF), V((tok, hg), BF), V((tok, hg), BF),
        V((tok, hg), BF), V((tok, hg), BF), V((tok, group), BF), V((tok, blk), F32), V((nch, 3, CHUNK, blk), BF), V((tok, half), BF),
        V((tok, feats), F32), V((tok, feats), F32), V((tok, feats), F32), V((tok, feats), BF), V((nch, 3, rows, feats), BF),
        V((nch, rows, feats), F32), V((nch, rows, feats), F32), V((tok, feats), BF), V((2 * feats, half), BF),
        V((8, feats), F32), V((3, 8, feats), F32), V((8, blk), F32), V((3, 8, blk), F32), V((3, 8, blk), F32), V((8, blk), F32),
        V((3, 8, blk), F32), V((8, blk), F32), V((8, blk), F32), V((8, blk), F32), V((8, blk), F32), V((8, blk), F32), V((8, blk), F32),
        pltpu.SemaphoreType.DMA((5,)), pltpu.SemaphoreType.DMA((len(KINDS),)), pltpu.SemaphoreType.DMA((len(KINDS), nch)),
        pltpu.SemaphoreType.DMA((len(ONCE),)), pltpu.SemaphoreType.DMA((len(ONCE),)),
    ]
    ge, geb, gd, gdb, loss = pl.pallas_call(
        kernel,
        out_shape=(
            jax.ShapeDtypeStruct((depth, feats), F32),
            jax.ShapeDtypeStruct((1, feats), F32),
            jax.ShapeDtypeStruct((1, feats, width), BF),
            jax.ShapeDtypeStruct((1, blk), F32),
            jax.ShapeDtypeStruct((1, 1), F32),
        ),
        in_specs=[any_spec, any_spec, vmem_spec, any_spec, vmem_spec, any_spec],
        out_specs=(vmem_spec, vmem_spec, any_spec, vmem_spec, pl.BlockSpec(memory_space=pltpu.SMEM)),
        scratch_shapes=scratch,
        compiler_params=pltpu.CompilerParams(collective_id=0, has_side_effects=True, vmem_limit_bytes=56 << 20),
    )(source, enc_weight, enc_bias.reshape(1, feats), dec_weight, dec_bias, target)
    return ge, geb.reshape(feats), gd, gdb, loss.reshape(())


def solution(mesh):
    return jax.shard_map(
        shards,
        mesh=mesh,
        in_specs=(
            P(None, "layer"),
            P("layer", "feat"),
            P("feat"),
            P("layer", "feat", None),
            P("layer", None),
            P("layer", None, None),
        ),
        out_specs=(
            P("layer", "feat"),
            P("feat"),
            P("layer", "feat", None),
            P("layer", "feat"),
            P(),
        ),
        check_vma=False,
    )
```

```python
import functools

import jax
import jax.numpy as jnp
from jax import lax
from jax.experimental import pallas as pl
from jax.experimental.pallas import tpu as pltpu
from jax.sharding import PartitionSpec as P

BF = jnp.bfloat16
F32 = jnp.float32
MESH = pl.DeviceIdType.MESH

NY, NX, NZ = 4, 4, 4
CHUNK = 64
STAGES = ("P1", "P2", "P3", "P4", "P5", "P6A", "P6", "P7", "P8", "P8A", "P9", "P10", "P11", "P12")
SCHEDULE = (
    0, 1, 2, 3, 17, 32, 4, 18, 33, 5, 19, 48, 34, 6, 64, 20, 49, 35, 7, 65,
    21, 50, 80, 36, 66, 22, 51, 81, 37, 96, 67, 23, 52, 82, 38, 97, 68, 53, 83, 39,
    112, 98, 69, 54, 84, 113, 99, 70, 128, 55, 85, 114, 100, 71, 129, 144, 86, 115, 101, 130,
    145, 87, 116, 160, 102, 131, 146, 176, 117, 161, 103, 132, 147, 177, 118, 162, 133, 148, 192, 178,
    119, 163, 134, 149, 193, 179, 164, 208, 135, 150, 194, 180, 165, 209, 195, 181, 166, 210, 196, 182,
    167, 211, 197, 183, 224, 225, 212, 198, 213, 214, 215,
)
PRE_DIRECT, BACK_DIRECT, X_DIRECT = (0,), (7,), (7,)
KINDS = ("YR", "ZP", "YA", "SA", "HP", "HM", "OP", "OM", "AP", "AM", "ZR", "ZA", "XP", "XM", "FP", "FM", "SB", "YB", "ZB", "YD", "D1", "D2", "X2")
ID = {name: i for i, name in enumerate(KINDS)}
ONCE = ("W", "GB", "L1", "L2", "L3", "L4", "L5", "GD")
OID = {name: i for i, name in enumerate(ONCE)}
A0 = 0.7978845608
A1 = 0.044715


def dot(a, b, dims):
    return lax.dot_general(a, b, (dims, ((), ())), preferred_element_type=F32)


def kernel(
    src_h, enc_h, encb_h, w_h, decb_h, tgt_h,
    ge_v, geb_v, gd_h, gdb_v, loss_s,
    src, enc, tgt, encb_v, decb_v, w, ps, ry, zs_p, zr_p, gpr, acts, rec, own, hp, hm, op, om, ap, am, sp, sm, zsend, zown, rz, eall,
    b_own, b_send, b_recv, by, ryb, zs_b, zr_b, dall, gd, pb, rpb, sq, rl1, rl2, rl3, rl4, rl5, sl2, sl3, sl4, sl5, bsum, psb, rd1, rd2,
    lsem, ssem, rsem, oss, ors,
):
    tok, depth = src.shape
    feats = enc.shape[1]
    half = w.shape[1]
    tt = CHUNK
    nch = tok // tt
    rows = tt // NY
    group = half // NX
    hg = group // 2
    blk = group // NZ
    lay, fea = lax.axis_index("layer"), lax.axis_index("feat")
    zl, y = lay // NY, lay % NY
    zh, x, core = fea // (2 * NX), (fea // 2) % NX, fea % 2

    def dev(dzl=0, dy=0, dzh=0, dx=0, dc=0):
        return (
            ((zl + dzl) % 2) * NY + (y + dy) % NY,
            ((zh + dzh) % NZ) * (2 * NX) + ((x + dx) % NX) * 2 + (core + dc) % 2,
        )

    def send(kind, k, src_ref, dst_ref, to):
        pltpu.make_async_remote_copy(
            src_ref, dst_ref, ssem.at[ID[kind]], rsem.at[ID[kind], k], device_id=to, device_id_type=MESH
        ).start()

    def got(kind, k, ref):
        pltpu.make_async_copy(ref, ref, rsem.at[ID[kind], k]).wait()

    def send1(kind, src_ref, dst_ref, to):
        pltpu.make_async_remote_copy(
            src_ref, dst_ref, oss.at[OID[kind]], ors.at[OID[kind]], device_id=to, device_id_type=MESH
        ).start()

    def got1(kind, ref):
        pltpu.make_async_copy(ref, ref, ors.at[OID[kind]]).wait()

    barrier = pltpu.get_barrier_semaphore()
    peers = (
        [dict(dzl=z, dy=o) for z in range(2) for o in range(NY) if z or o] + [dict(dc=1)]
        + [dict(dx=o) for o in range(1, NX)] + [dict(dzh=o) for o in range(1, NZ)]
    )
    for p in peers:
        pl.semaphore_signal(barrier, inc=1, device_id=dev(**p), device_id_type=MESH)

    c_src = pltpu.make_async_copy(src_h, src, lsem.at[0])
    c_enc = pltpu.make_async_copy(enc_h, enc, lsem.at[1])
    c_src.start()
    c_enc.start()

    def column(o, p, c):
        return pl.multiple_of((((zh + p) % NZ) * (2 * NX) + ((x + o) % NX) * 2 + c) * blk, blk)

    for o in range(NX):
        for p in range(NZ):
            pltpu.make_async_copy(
                w_h.at[0, :, pl.ds(column(o, p, core), blk)],
                w.at[pl.ds(0, feats), pl.ds((o * NZ + p) * blk, blk)],
                lsem.at[2],
            ).start()
    c_tgt = pltpu.make_async_copy(tgt_h.at[0, :, pl.ds(pl.multiple_of(fea * blk, blk), blk)], tgt, lsem.at[3])
    c_tgt.start()
    c_encb = pltpu.make_async_copy(encb_h, encb_v, lsem.at[5])
    c_encb.start()
    c_decb = pltpu.make_async_copy(decb_h.at[:, pl.ds(pl.multiple_of(fea * blk, blk), blk)], decb_v, lsem.at[6])
    c_decb.start()
    c_src.wait()
    c_enc.wait()
    c_encb.wait()
    ps[...] = dot(src[...], enc[...], ((1,), (0,)))
    pl.semaphore_wait(barrier, len(peers))
    for o in range(NX):
        for p in range(NZ):
            send1(
                "W", w_h.at[0, :, pl.ds(column(o, p, 1 - core), blk)],
                w.at[pl.ds(feats, feats), pl.ds((o * NZ + p) * blk, blk)], dev(dc=1),
            )
    sq[...] = jnp.zeros_like(sq)
    pb[...] = jnp.zeros_like(pb)
    bsum[...] = jnp.zeros_like(bsum)

    def span(k):
        return pl.ds(k * tt, tt)

    def piece(k, yy):
        return pl.ds(pl.multiple_of(k * tt + yy * rows, rows), rows)

    def fold(v):
        return jnp.sum(v.reshape(v.shape[0] // 8, 8, v.shape[1]), axis=0)

    def everyone(kind, k, buf, slots):
        slots[lay] = buf[piece(k, y)]
        for dzl in range(2):
            for o in range(NY):
                if dzl or o:
                    send(kind, k, buf.at[piece(k, (y + o) % NY)], slots.at[lay], dev(dzl=dzl, dy=o))

    def total(slots):
        v = slots[0].astype(F32)
        for i in range(1, 2 * NY):
            v = v + slots[i].astype(F32)
        return v

    def p1(k):
        if k in PRE_DIRECT:
            psb[span(k)] = ps[span(k)].astype(BF)
            everyone("D1", k, psb, rd1.at[k])
            return
        for o in range(1, NY):
            send("YR", k, ps.at[piece(k, (y + o) % NY)], ry.at[k, o - 1], dev(dy=o))

    def p2(k):
        got("YR", k, ry.at[k])
        zs_p[k] = ps[piece(k, y)] + ry[k, 0] + ry[k, 1] + ry[k, 2]
        send("ZP", k, zs_p.at[k], zr_p.at[k], dev(dzl=1))

    def p3(k):
        if k in PRE_DIRECT:
            got("D1", k, rd1.at[k, pl.ds(0, 2 * NY - 1)])
            v = total(rd1.at[k]) + encb_v[...]
        else:
            got("ZP", k, zr_p.at[k])
            v = zs_p[k] + zr_p[k] + encb_v[...]
        v2 = v * v
        t = jnp.tanh(A0 * (v * (1.0 + A1 * v2)))
        h = 0.5 * (1.0 + t)
        acts[piece(k, y), pl.ds(0, feats)] = (v * h).astype(BF)
        for o in range(1, NY):
            r = acts.at[piece(k, y), pl.ds(0, feats)]
            send("YA", k, r, r, dev(dy=o))
        gpr[k] = h + 0.5 * v * (1.0 - t * t) * (A0 * (1.0 + 3.0 * A1 * v2))

    def p4(k):
        got("YA", k, acts.at[pl.ds(0, 3 * rows), pl.ds(0, feats)])
        send("SA", k, acts.at[span(k), pl.ds(0, feats)], acts.at[span(k), pl.ds(feats, feats)], dev(dc=1))

    def p5(k):
        got("SA", k, acts.at[span(k), pl.ds(feats, feats)])

        if k == 0:
            pltpu.make_async_copy(w.at[pl.ds(0, feats)], w.at[pl.ds(0, feats)], lsem.at[2]).wait()
            got1("W", w.at[pl.ds(feats, feats)])

        a = acts[span(k)]
        s = span(k)
        for o in (2, 1, 3):
            rec[s, pl.ds(o * group, group)] = dot(a, w[:, pl.ds(o * group, group)], ((1,), (0,))).astype(BF)
            if o == 2:
                send("HP", k, rec.at[s, pl.ds(2 * group, hg)], hp.at[s], dev(dx=1))
                send("HM", k, rec.at[s, pl.ds(2 * group + hg, hg)], hm.at[s], dev(dx=3))
            elif o == 1:
                send("OP", k, rec.at[s, pl.ds(group + hg, hg)], op.at[s], dev(dx=1))
            else:
                send("OM", k, rec.at[s, pl.ds(3 * group, hg)], om.at[s], dev(dx=3))
        own[s] = dot(a, w[:, pl.ds(0, group)], ((1,), (0,)))

    def p6a(k):
        s = span(k)
        got("HP", k, hp.at[s])
        sp[s] = (hp[s].astype(F32) + rec[s, pl.ds(group, hg)].astype(F32)).astype(BF)
        send("AP", k, sp.at[s], ap.at[s], dev(dx=1))
        got("HM", k, hm.at[s])
        sm[s] = (hm[s].astype(F32) + rec[s, pl.ds(3 * group + hg, hg)].astype(F32)).astype(BF)
        send("AM", k, sm.at[s], am.at[s], dev(dx=3))

    def p6(k):
        s = span(k)
        got("OP", k, op.at[s])
        got("OM", k, om.at[s])
        got("AP", k, ap.at[s])
        got("AM", k, am.at[s])
        first = own[s, pl.ds(0, hg)] + ap[s].astype(F32) + om[s].astype(F32)
        second = own[s, pl.ds(hg, hg)] + am[s].astype(F32) + op[s].astype(F32)
        zown[s] = first[:, :blk]
        zsend[s, pl.ds(0, hg)] = first.astype(BF)
        zsend[s, pl.ds(hg, hg)] = second.astype(BF)
        for p in range(1, NZ):
            send("ZR", k, zsend.at[s, pl.ds(p * blk, blk)], rz.at[k, p - 1], dev(dzh=p))

    def p7(k):
        s = span(k)
        got("ZR", k, rz.at[k])
        recon = zown[s] + rz[k, 0].astype(F32) + rz[k, 1].astype(F32) + rz[k, 2].astype(F32)

        if k == 0:
            c_tgt.wait()
            c_decb.wait()

        err = recon + decb_v[...] - tgt[s].astype(F32)
        eall[s, pl.ds(0, blk)] = err.astype(BF)
        for p in range(1, NZ):
            send("ZA", k, eall.at[s, pl.ds(0, blk)], eall.at[s, pl.ds((NZ - p) * blk, blk)], dev(dzh=p))
        bsum[...] += fold(err)
        sq[...] += fold(err * err)

    def p8(k):
        s = span(k)
        got("ZA", k, eall.at[s, pl.ds(blk, 3 * blk)])
        send("XP", k, eall.at[s, pl.ds(0, group)], eall.at[s, pl.ds(3 * group, group)], dev(dx=1))
        send("XM", k, eall.at[s, pl.ds(0, group)], eall.at[s, pl.ds(group, group)], dev(dx=3))
        if k in X_DIRECT:
            send("X2", k, eall.at[s, pl.ds(0, group)], eall.at[s, pl.ds(2 * group, group)], dev(dx=2))

    def p8a(k):
        s = span(k)
        got("XP", k, eall.at[s, pl.ds(3 * group, group)])
        send("FP", k, eall.at[s, pl.ds(3 * group, hg)], eall.at[s, pl.ds(2 * group, hg)], dev(dx=1))
        got("XM", k, eall.at[s, pl.ds(group, group)])
        send("FM", k, eall.at[s, pl.ds(group + hg, hg)], eall.at[s, pl.ds(2 * group + hg, hg)], dev(dx=3))

    def p9(k):
        s = span(k)
        if k in X_DIRECT:
            got("XP", k, eall.at[s, pl.ds(3 * group, group)])
            got("XM", k, eall.at[s, pl.ds(group, group)])
            got("X2", k, eall.at[s, pl.ds(2 * group, group)])
        else:
            got("FP", k, eall.at[s, pl.ds(2 * group, hg)])
            got("FM", k, eall.at[s, pl.ds(2 * group + hg, hg)])
        e = eall[s]
        b_send[s] = dot(e, w[pl.ds(feats, feats)], ((1,), (1,)))
        send("SB", k, b_send.at[s], b_recv.at[s], dev(dc=1))
        b_own[s] = dot(e, w[pl.ds(0, feats)], ((1,), (1,)))

    def p10(k):
        s = span(k)
        got("SB", k, b_recv.at[s])
        by[s] = (b_own[s] + b_recv[s]).astype(BF)
        if k in BACK_DIRECT:
            everyone("D2", k, by, rd2.at[k])
            return
        for o in range(1, NY):
            send("YB", k, by.at[piece(k, (y + o) % NY)], ryb.at[k, o - 1], dev(dy=o))

    def p11(k):
        got("YB", k, ryb.at[k])
        me = piece(k, y)
        zs_b[k] = (
            b_own[me] + b_recv[me] + ryb[k, 0].astype(F32) + ryb[k, 1].astype(F32) + ryb[k, 2].astype(F32)
        )
        send("ZB", k, zs_b.at[k], zr_b.at[k], dev(dzl=1))

    def p12(k):
        if k in BACK_DIRECT:
            got("D2", k, rd2.at[k, pl.ds(0, 2 * NY - 1)])
            dpre = total(rd2.at[k]) * gpr[k]
        else:
            got("ZB", k, zr_b.at[k])
            dpre = (zs_b[k] + zr_b[k]) * gpr[k]
        r = dall.at[piece(k, y)]
        dall[piece(k, y)] = dpre.astype(BF)
        for o in range(1, NY):
            send("YD", k, r, r, dev(dy=o))
        pb[...] += fold(dpre)

        if k == nch - 1:
            for o in range(1, NY):
                send1("GB", pb, rpb.at[o - 1], dev(dy=o))

    def p13(k):
        got("YD", k, dall.at[pl.ds(0, 3 * rows)])

    stages = dict(P1=p1, P2=p2, P3=p3, P4=p4, P5=p5, P6A=p6a, P6=p6, P7=p7, P8=p8, P8A=p8a, P9=p9, P10=p10, P11=p11, P12=p12)

    def grad(base, which):
        def body(n, _):
            at = pl.multiple_of(n * group, group)
            gd[pl.ds(base, feats), pl.ds(at, group)] = dot(
                acts[:, pl.ds(base, feats)], eall[:, pl.ds(at, group)], ((0,), (0,))
            ).astype(BF)
            for p in range(NZ):
                part = gd.at[pl.ds(base, feats), pl.ds(pl.multiple_of(at + p * blk, blk), blk)]
                where = gd_h.at[0, :, pl.ds(column(n, p, core), blk)]
                if which:
                    send1("GD", part, where, dev(dc=1))
                else:
                    pltpu.make_async_copy(part, where, lsem.at[4]).start()
            return 0

        lax.fori_loop(0, NX, body, 0)

    def l1():
        for o in range(1, NZ):
            send1("L1", sq, rl1.at[o - 1], dev(dzh=o))

    def l2():
        got1("L1", rl1)
        sl2[...] = sq[...] + rl1[0] + rl1[1] + rl1[2]
        for o in range(1, NX):
            send1("L2", sl2, rl2.at[o - 1], dev(dx=o))

    def l3():
        got1("L2", rl2)
        sl3[...] = sl2[...] + rl2[0] + rl2[1] + rl2[2]
        send1("L3", sl3, rl3, dev(dc=1))

    def l4():
        got1("L3", rl3)
        sl4[...] = sl3[...] + rl3[...]
        for o in range(1, NY):
            send1("L4", sl4, rl4.at[o - 1], dev(dy=o))

    def l5():
        got1("L4", rl4)
        sl5[...] = sl4[...] + rl4[0] + rl4[1] + rl4[2]
        send1("L5", sl5, rl5, dev(dzl=1))

    last = nch - 1
    side = {"P7": l1, "P8": l2, "P9": l3, "P10": l4, "P12": l5}
    for code in SCHEDULE:
        stage, k = code // 16, code % 16
        if stage == len(STAGES):
            grad(feats * (1 - k), k == 0)
            continue
        name = STAGES[stage]
        stages[name](k)
        if k == last and name in side:
            side[name]()

    for k in range(nch):
        p13(k)
    ge_v[...] = dot(src[...], dall[...], ((0,), (0,)))
    got1("GB", rpb)
    geb_v[...] = jnp.sum(pb[...] + rpb[0] + rpb[1] + rpb[2], axis=0, keepdims=True)
    gdb_v[...] = jnp.sum(bsum[...], axis=0, keepdims=True)
    got1("L5", rl5)
    layers = 2 * NY
    width = 2 * half
    loss_s[0, 0] = jnp.sum(sl5[...] + rl5[...]) / (2.0 * tok * layers * width)

    own_gd = gd.at[pl.ds(0, feats)]
    pltpu.make_async_copy(own_gd, own_gd, lsem.at[4]).wait()
    got1("GD", own_gd)
    def drain(kind, ref, only=None, skip=()):
        for k in range(nch) if only is None else only:
            if k not in skip:
                r = ref(k)
                pltpu.make_async_copy(r, r, ssem.at[ID[kind]]).wait()

    most = 2 * NY - 1
    drain("YR", lambda k: ry.at[k], skip=PRE_DIRECT)
    drain("ZP", lambda k: zr_p.at[k], skip=PRE_DIRECT)
    drain("D1", lambda k: rd1.at[k, pl.ds(0, most)], only=PRE_DIRECT)
    drain("YB", lambda k: ryb.at[k], skip=BACK_DIRECT)
    drain("ZB", lambda k: zr_b.at[k], skip=BACK_DIRECT)
    drain("D2", lambda k: rd2.at[k, pl.ds(0, most)], only=BACK_DIRECT)
    drain("FP", lambda k: hp.at[span(k)], skip=X_DIRECT)
    drain("FM", lambda k: hm.at[span(k)], skip=X_DIRECT)
    drain("X2", lambda k: eall.at[span(k), pl.ds(0, group)], only=X_DIRECT)
    q3 = 3 * tok // 4
    left = dict(
        YA=acts.at[pl.ds(0, q3), pl.ds(0, feats)], SA=acts.at[:, pl.ds(0, feats)], HP=hp, HM=hm, OP=op, OM=om, AP=ap, AM=am,
        ZR=rz, ZA=eall.at[:, pl.ds(0, 3 * blk)], XP=eall.at[:, pl.ds(0, group)], XM=eall.at[:, pl.ds(0, group)], SB=b_recv,
        YD=dall.at[pl.ds(0, q3)],
    )
    for name, ref in left.items():
        pltpu.make_async_copy(ref, ref, ssem.at[ID[name]]).wait()
    once = dict(W=w.at[pl.ds(0, feats)], GB=rpb, L1=rl1, L2=rl2, L3=rl3, L4=rl4, L5=rl5, GD=own_gd)
    for name, ref in once.items():
        pltpu.make_async_copy(ref, ref, oss.at[OID[name]]).wait()


def place(a, b, c, d, ao, bo, co, do, sem):
    copies = [pltpu.make_async_copy(i, o, sem.at[n]) for n, (i, o) in enumerate(((a, ao), (b, bo), (c, co), (d, do)))]
    for copy in copies:
        copy.start()
    for copy in copies:
        copy.wait()


def shards(source, enc_weight, enc_bias, dec_weight, dec_bias, target):
    tok, depth = source.shape
    feats = enc_weight.shape[1]
    width = dec_weight.shape[2]
    half = width // 2
    group = half // NX
    hg = group // 2
    blk = group // NZ
    nch = tok // CHUNK
    rows = CHUNK // NY
    V = pltpu.VMEM
    any_spec = pl.BlockSpec(memory_space=pl.ANY)
    hbm_spec = pl.BlockSpec(memory_space=pltpu.HBM)
    vmem_spec = pl.BlockSpec(memory_space=pltpu.VMEM)
    scratch = [
        V((tok, depth), BF), V((depth, feats), BF), V((tok, blk), BF), V((1, feats), F32), V((1, blk), F32), V((2 * feats, half), BF),
        V((tok, feats), F32), V((nch, 3, rows, feats), F32), V((nch, rows, feats), F32), V((nch, rows, feats), F32),
        V((nch, rows, feats), F32), V((tok, 2 * feats), BF), V((tok, half), BF), V((tok, group), F32),
        V((tok, hg), BF), V((tok, hg), BF), V((tok, hg), BF), V((tok, hg), BF), V((tok, hg), BF), V((tok, hg), BF),
        V((tok, hg), BF), V((tok, hg), BF), V((tok, group), BF), V((tok, blk), F32), V((nch, 3, CHUNK, blk), BF), V((tok, half), BF),
        V((tok, feats), F32), V((tok, feats), F32), V((tok, feats), F32), V((tok, feats), BF), V((nch, 3, rows, feats), BF),
        V((nch, rows, feats), F32), V((nch, rows, feats), F32), V((tok, feats), BF), V((2 * feats, half), BF),
        V((8, feats), F32), V((3, 8, feats), F32), V((8, blk), F32), V((3, 8, blk), F32), V((3, 8, blk), F32), V((8, blk), F32),
        V((3, 8, blk), F32), V((8, blk), F32), V((8, blk), F32), V((8, blk), F32), V((8, blk), F32), V((8, blk), F32), V((8, blk), F32),
        V((tok, feats), BF), V((nch, 2 * NY, rows, feats), BF), V((nch, 2 * NY, rows, feats), BF),
        pltpu.SemaphoreType.DMA((7,)), pltpu.SemaphoreType.DMA((len(KINDS),)), pltpu.SemaphoreType.DMA((len(KINDS), nch)),
        pltpu.SemaphoreType.DMA((len(ONCE),)), pltpu.SemaphoreType.DMA((len(ONCE),)),
    ]
    ge, geb, gd, gdb, loss = pl.pallas_call(
        kernel,
        out_shape=(
            jax.ShapeDtypeStruct((depth, feats), F32),
            jax.ShapeDtypeStruct((1, feats), F32),
            jax.ShapeDtypeStruct((1, feats, width), BF),
            jax.ShapeDtypeStruct((1, blk), F32),
            jax.ShapeDtypeStruct((1, 1), F32),
        ),
        in_specs=[any_spec] * 6,
        out_specs=(vmem_spec, vmem_spec, any_spec, vmem_spec, pl.BlockSpec(memory_space=pltpu.SMEM)),
        scratch_shapes=scratch,
        compiler_params=pltpu.CompilerParams(collective_id=0, has_side_effects=True, vmem_limit_bytes=45 << 20),
    )(*(pltpu.with_memory_space_constraint(v, pltpu.HBM) for v in (source, enc_weight, enc_bias.reshape(1, feats), dec_weight, dec_bias, target)))
    outs = (ge, geb, gd, gdb)
    ge, geb, gd, gdb = pl.pallas_call(
        place,
        out_shape=tuple(pltpu.HBM(v.shape, v.dtype) for v in outs),
        in_specs=[any_spec] * 4,
        out_specs=(any_spec,) * 4,
        scratch_shapes=[pltpu.SemaphoreType.DMA((4,))],
        compiler_params=pltpu.CompilerParams(vmem_limit_bytes=1 << 20),
    )(*(pltpu.with_memory_space_constraint(v, pltpu.VMEM) for v in outs))
    return ge, geb.reshape(feats), gd, gdb, loss.reshape(())


def solution(mesh):
    return jax.shard_map(
        shards,
        mesh=mesh,
        in_specs=(
            P(None, "layer"),
            P("layer", "feat"),
            P("feat"),
            P("layer", "feat", None),
            P("layer", None),
            P("layer", None, None),
        ),
        out_specs=(
            P("layer", "feat"),
            P("feat"),
            P("layer", "feat", None),
            P("layer", "feat"),
            P(),
        ),
        check_vma=False,
    )
```

```python
import functools

import jax
import jax.numpy as jnp
from jax import lax
from jax.experimental import pallas as pl
from jax.experimental.pallas import tpu as pltpu
from jax.sharding import PartitionSpec as P

BF = jnp.bfloat16
F32 = jnp.float32
MESH = pl.DeviceIdType.MESH

NY, NX, NZ = 4, 4, 4
CHUNK = 64
STAGES = ("P1", "P2", "P3", "P4", "P5", "P6A", "P6", "P7", "P8", "P8A", "P9", "P10", "P11", "P12")
SCHEDULE = (
    2, 0, 1, 18, 5, 32, 17, 34, 3, 48, 6, 21, 33, 64, 50, 37, 19, 4, 66, 49,
    22, 80, 7, 35, 65, 53, 82, 20, 38, 96, 69, 23, 81, 51, 36, 98, 67, 54, 85, 39,
    97, 52, 112, 70, 83, 101, 114, 55, 68, 86, 113, 71, 99, 84, 128, 102, 117, 130, 87, 100,
    144, 115, 129, 146, 103, 133, 118, 160, 145, 116, 131, 162, 149, 176, 119, 134, 161, 147, 178, 132,
    165, 192, 150, 177, 181, 135, 163, 194, 148, 208, 166, 179, 197, 193, 210, 182, 164, 167, 180, 195,
    213, 198, 183, 224, 196, 209, 211, 214, 215, 212, 225,
)
PRE_DIRECT, BACK_DIRECT, X_DIRECT = (0,), (7,), (7,)
KINDS = ("YR", "ZP", "YA", "SA", "HP", "HM", "OP", "OM", "AP", "AM", "ZR", "ZA", "XP", "XM", "FP", "FM", "SB", "YB", "ZB", "YD", "D1", "D2", "X2")
ID = {name: i for i, name in enumerate(KINDS)}
ONCE = ("W", "GB", "L1", "L2", "L3", "L4", "L5", "GD")
OID = {name: i for i, name in enumerate(ONCE)}
A0 = 0.7978845608
A1 = 0.044715


def dot(a, b, dims):
    return lax.dot_general(a, b, (dims, ((), ())), preferred_element_type=F32)


def kernel(
    src_h, enc_h, encb_h, w_h, decb_h, tgt_h,
    ge_v, geb_v, gd_h, gdb_v, loss_s,
    src, enc, tgt, encb_v, decb_v, w, ps, ry, zs_p, zr_p, gpr, acts, rec, own, hp, hm, op, om, ap, am, sp, sm, zsend, zown, rz, eall,
    b_own, b_send, b_recv, by, ryb, zs_b, zr_b, dall, gd, pb, rpb, sq, rl1, rl2, rl3, rl4, rl5, sl2, sl3, sl4, sl5, bsum, psb, rd1, rd2,
    lsem, ssem, rsem, oss, ors,
):
    tok, depth = src.shape
    feats = enc.shape[1]
    half = w.shape[1]
    tt = CHUNK
    nch = tok // tt
    rows = tt // NY
    group = half // NX
    hg = group // 2
    blk = group // NZ
    lay, fea = lax.axis_index("layer"), lax.axis_index("feat")
    zl, y = lay // NY, lay % NY
    zh, x, core = fea // (2 * NX), (fea // 2) % NX, fea % 2

    def dev(dzl=0, dy=0, dzh=0, dx=0, dc=0):
        return (
            ((zl + dzl) % 2) * NY + (y + dy) % NY,
            ((zh + dzh) % NZ) * (2 * NX) + ((x + dx) % NX) * 2 + (core + dc) % 2,
        )

    def send(kind, k, src_ref, dst_ref, to):
        pltpu.make_async_remote_copy(
            src_ref, dst_ref, ssem.at[ID[kind]], rsem.at[ID[kind], k], device_id=to, device_id_type=MESH
        ).start()

    def got(kind, k, ref):
        pltpu.make_async_copy(ref, ref, rsem.at[ID[kind], k]).wait()

    def send1(kind, src_ref, dst_ref, to):
        pltpu.make_async_remote_copy(
            src_ref, dst_ref, oss.at[OID[kind]], ors.at[OID[kind]], device_id=to, device_id_type=MESH
        ).start()

    def got1(kind, ref):
        pltpu.make_async_copy(ref, ref, ors.at[OID[kind]]).wait()

    barrier = pltpu.get_barrier_semaphore()
    peers = (
        [dict(dzl=z, dy=o) for z in range(2) for o in range(NY) if z or o] + [dict(dc=1)]
        + [dict(dx=o) for o in range(1, NX)] + [dict(dzh=o) for o in range(1, NZ)]
    )
    for p in peers:
        pl.semaphore_signal(barrier, inc=1, device_id=dev(**p), device_id_type=MESH)

    c_src = pltpu.make_async_copy(src_h, src, lsem.at[0])
    c_enc = pltpu.make_async_copy(enc_h, enc, lsem.at[1])
    c_src.start()
    c_enc.start()

    def column(o, p, c):
        return pl.multiple_of((((zh + p) % NZ) * (2 * NX) + ((x + o) % NX) * 2 + c) * blk, blk)

    for o in range(NX):
        for p in range(NZ):
            pltpu.make_async_copy(
                w_h.at[0, :, pl.ds(column(o, p, core), blk)],
                w.at[pl.ds(0, feats), pl.ds((o * NZ + p) * blk, blk)],
                lsem.at[2],
            ).start()
    c_tgt = pltpu.make_async_copy(tgt_h.at[0, :, pl.ds(pl.multiple_of(fea * blk, blk), blk)], tgt, lsem.at[3])
    c_tgt.start()
    c_encb = pltpu.make_async_copy(encb_h, encb_v, lsem.at[5])
    c_encb.start()
    c_decb = pltpu.make_async_copy(decb_h.at[:, pl.ds(pl.multiple_of(fea * blk, blk), blk)], decb_v, lsem.at[6])
    c_decb.start()
    c_src.wait()
    c_enc.wait()
    c_encb.wait()
    ps[...] = dot(src[...], enc[...], ((1,), (0,)))
    pl.semaphore_wait(barrier, len(peers))
    for o in range(NX):
        for p in range(NZ):
            send1(
                "W", w_h.at[0, :, pl.ds(column(o, p, 1 - core), blk)],
                w.at[pl.ds(feats, feats), pl.ds((o * NZ + p) * blk, blk)], dev(dc=1),
            )
    sq[...] = jnp.zeros_like(sq)
    pb[...] = jnp.zeros_like(pb)
    bsum[...] = jnp.zeros_like(bsum)

    def span(k):
        return pl.ds(k * tt, tt)

    def piece(k, yy):
        return pl.ds(pl.multiple_of(k * tt + yy * rows, rows), rows)

    def fold(v):
        return jnp.sum(v.reshape(v.shape[0] // 8, 8, v.shape[1]), axis=0)

    def everyone(kind, k, buf, slots):
        slots[lay] = buf[piece(k, y)]
        for dzl in range(2):
            for o in range(NY):
                if dzl or o:
                    send(kind, k, buf.at[piece(k, (y + o) % NY)], slots.at[lay], dev(dzl=dzl, dy=o))

    def total(slots):
        v = slots[0].astype(F32)
        for i in range(1, 2 * NY):
            v = v + slots[i].astype(F32)
        return v

    def p1(k):
        if k in PRE_DIRECT:
            psb[span(k)] = ps[span(k)].astype(BF)
            everyone("D1", k, psb, rd1.at[k])
            return
        for o in range(1, NY):
            send("YR", k, ps.at[piece(k, (y + o) % NY)], ry.at[k, o - 1], dev(dy=o))

    def p2(k):
        got("YR", k, ry.at[k])
        zs_p[k] = ps[piece(k, y)] + ry[k, 0] + ry[k, 1] + ry[k, 2]
        send("ZP", k, zs_p.at[k], zr_p.at[k], dev(dzl=1))

    def p3(k):
        if k in PRE_DIRECT:
            got("D1", k, rd1.at[k, pl.ds(0, 2 * NY - 1)])
            v = total(rd1.at[k]) + encb_v[...]
        else:
            got("ZP", k, zr_p.at[k])
            v = zs_p[k] + zr_p[k] + encb_v[...]
        v2 = v * v
        t = jnp.tanh(A0 * (v * (1.0 + A1 * v2)))
        h = 0.5 * (1.0 + t)
        acts[piece(k, y), pl.ds(0, feats)] = (v * h).astype(BF)
        for o in range(1, NY):
            r = acts.at[piece(k, y), pl.ds(0, feats)]
            send("YA", k, r, r, dev(dy=o))
        gpr[k] = h + 0.5 * v * (1.0 - t * t) * (A0 * (1.0 + 3.0 * A1 * v2))

    def p4(k):
        got("YA", k, acts.at[pl.ds(0, 3 * rows), pl.ds(0, feats)])
        send("SA", k, acts.at[span(k), pl.ds(0, feats)], acts.at[span(k), pl.ds(feats, feats)], dev(dc=1))

    def p5(k):
        got("SA", k, acts.at[span(k), pl.ds(feats, feats)])

        if k == 0:
            pltpu.make_async_copy(w.at[pl.ds(0, feats)], w.at[pl.ds(0, feats)], lsem.at[2]).wait()
            got1("W", w.at[pl.ds(feats, feats)])

        a = acts[span(k)]
        s = span(k)
        for o in (2, 1, 3):
            rec[s, pl.ds(o * group, group)] = dot(a, w[:, pl.ds(o * group, group)], ((1,), (0,))).astype(BF)
            if o == 2:
                send("HP", k, rec.at[s, pl.ds(2 * group, hg)], hp.at[s], dev(dx=1))
                send("HM", k, rec.at[s, pl.ds(2 * group + hg, hg)], hm.at[s], dev(dx=3))
            elif o == 1:
                send("OP", k, rec.at[s, pl.ds(group + hg, hg)], op.at[s], dev(dx=1))
            else:
                send("OM", k, rec.at[s, pl.ds(3 * group, hg)], om.at[s], dev(dx=3))
        own[s] = dot(a, w[:, pl.ds(0, group)], ((1,), (0,)))

    def p6a(k):
        s = span(k)
        got("HP", k, hp.at[s])
        sp[s] = (hp[s].astype(F32) + rec[s, pl.ds(group, hg)].astype(F32)).astype(BF)
        send("AP", k, sp.at[s], ap.at[s], dev(dx=1))
        got("HM", k, hm.at[s])
        sm[s] = (hm[s].astype(F32) + rec[s, pl.ds(3 * group + hg, hg)].astype(F32)).astype(BF)
        send("AM", k, sm.at[s], am.at[s], dev(dx=3))

    def p6(k):
        s = span(k)
        got("OP", k, op.at[s])
        got("OM", k, om.at[s])
        got("AP", k, ap.at[s])
        got("AM", k, am.at[s])
        first = own[s, pl.ds(0, hg)] + ap[s].astype(F32) + om[s].astype(F32)
        second = own[s, pl.ds(hg, hg)] + am[s].astype(F32) + op[s].astype(F32)
        zown[s] = first[:, :blk]
        zsend[s, pl.ds(0, hg)] = first.astype(BF)
        zsend[s, pl.ds(hg, hg)] = second.astype(BF)
        for p in range(1, NZ):
            send("ZR", k, zsend.at[s, pl.ds(p * blk, blk)], rz.at[k, p - 1], dev(dzh=p))

    def p7(k):
        s = span(k)
        got("ZR", k, rz.at[k])
        recon = zown[s] + rz[k, 0].astype(F32) + rz[k, 1].astype(F32) + rz[k, 2].astype(F32)

        if k == 0:
            c_tgt.wait()
            c_decb.wait()

        err = recon + decb_v[...] - tgt[s].astype(F32)
        eall[s, pl.ds(0, blk)] = err.astype(BF)
        for p in range(1, NZ):
            send("ZA", k, eall.at[s, pl.ds(0, blk)], eall.at[s, pl.ds((NZ - p) * blk, blk)], dev(dzh=p))
        bsum[...] += fold(err)
        sq[...] += fold(err * err)

    def p8(k):
        s = span(k)
        got("ZA", k, eall.at[s, pl.ds(blk, 3 * blk)])
        send("XP", k, eall.at[s, pl.ds(0, group)], eall.at[s, pl.ds(3 * group, group)], dev(dx=1))
        send("XM", k, eall.at[s, pl.ds(0, group)], eall.at[s, pl.ds(group, group)], dev(dx=3))
        if k in X_DIRECT:
            send("X2", k, eall.at[s, pl.ds(0, group)], eall.at[s, pl.ds(2 * group, group)], dev(dx=2))

    def p8a(k):
        s = span(k)
        got("XP", k, eall.at[s, pl.ds(3 * group, group)])
        send("FP", k, eall.at[s, pl.ds(3 * group, hg)], eall.at[s, pl.ds(2 * group, hg)], dev(dx=1))
        got("XM", k, eall.at[s, pl.ds(group, group)])
        send("FM", k, eall.at[s, pl.ds(group + hg, hg)], eall.at[s, pl.ds(2 * group + hg, hg)], dev(dx=3))

    def p9(k):
        s = span(k)
        if k in X_DIRECT:
            got("XP", k, eall.at[s, pl.ds(3 * group, group)])
            got("XM", k, eall.at[s, pl.ds(group, group)])
            got("X2", k, eall.at[s, pl.ds(2 * group, group)])
        else:
            got("FP", k, eall.at[s, pl.ds(2 * group, hg)])
            got("FM", k, eall.at[s, pl.ds(2 * group + hg, hg)])
        e = eall[s]
        b_send[s] = dot(e, w[pl.ds(feats, feats)], ((1,), (1,)))
        send("SB", k, b_send.at[s], b_recv.at[s], dev(dc=1))
        b_own[s] = dot(e, w[pl.ds(0, feats)], ((1,), (1,)))

    def p10(k):
        s = span(k)
        got("SB", k, b_recv.at[s])
        by[s] = (b_own[s] + b_recv[s]).astype(BF)
        if k in BACK_DIRECT:
            everyone("D2", k, by, rd2.at[k])
            return
        for o in range(1, NY):
            send("YB", k, by.at[piece(k, (y + o) % NY)], ryb.at[k, o - 1], dev(dy=o))

    def p11(k):
        got("YB", k, ryb.at[k])
        me = piece(k, y)
        zs_b[k] = (
            b_own[me] + b_recv[me] + ryb[k, 0].astype(F32) + ryb[k, 1].astype(F32) + ryb[k, 2].astype(F32)
        )
        send("ZB", k, zs_b.at[k], zr_b.at[k], dev(dzl=1))

    def p12(k):
        if k in BACK_DIRECT:
            got("D2", k, rd2.at[k, pl.ds(0, 2 * NY - 1)])
            dpre = total(rd2.at[k]) * gpr[k]
        else:
            got("ZB", k, zr_b.at[k])
            dpre = (zs_b[k] + zr_b[k]) * gpr[k]
        r = dall.at[piece(k, y)]
        dall[piece(k, y)] = dpre.astype(BF)
        for o in range(1, NY):
            send("YD", k, r, r, dev(dy=o))
        pb[...] += fold(dpre)


    def p13(k):
        got("YD", k, dall.at[pl.ds(0, 3 * rows)])

    stages = dict(P1=p1, P2=p2, P3=p3, P4=p4, P5=p5, P6A=p6a, P6=p6, P7=p7, P8=p8, P8A=p8a, P9=p9, P10=p10, P11=p11, P12=p12)

    def grad(base, which):
        def body(n, _):
            at = pl.multiple_of(n * group, group)
            gd[pl.ds(base, feats), pl.ds(at, group)] = dot(
                acts[:, pl.ds(base, feats)], eall[:, pl.ds(at, group)], ((0,), (0,))
            ).astype(BF)
            for p in range(NZ):
                part = gd.at[pl.ds(base, feats), pl.ds(pl.multiple_of(at + p * blk, blk), blk)]
                where = gd_h.at[0, :, pl.ds(column(n, p, core), blk)]
                if which:
                    send1("GD", part, where, dev(dc=1))
                else:
                    pltpu.make_async_copy(part, where, lsem.at[4]).start()
            return 0

        lax.fori_loop(0, NX, body, 0)

    def bias():
        for o in range(1, NY):
            send1("GB", pb, rpb.at[o - 1], dev(dy=o))

    def l1():
        for o in range(1, NZ):
            send1("L1", sq, rl1.at[o - 1], dev(dzh=o))

    def l2():
        got1("L1", rl1)
        sl2[...] = sq[...] + rl1[0] + rl1[1] + rl1[2]
        for o in range(1, NX):
            send1("L2", sl2, rl2.at[o - 1], dev(dx=o))

    def l3():
        got1("L2", rl2)
        sl3[...] = sl2[...] + rl2[0] + rl2[1] + rl2[2]
        send1("L3", sl3, rl3, dev(dc=1))

    def l4():
        got1("L3", rl3)
        sl4[...] = sl3[...] + rl3[...]
        for o in range(1, NY):
            send1("L4", sl4, rl4.at[o - 1], dev(dy=o))

    def l5():
        got1("L4", rl4)
        sl5[...] = sl4[...] + rl4[0] + rl4[1] + rl4[2]
        send1("L5", sl5, rl5, dev(dzl=1))

    side = {"P7": (l1,), "P8": (l2,), "P9": (l3,), "P10": (l4,), "P12": (bias, l5)}
    left_of = [sum(c // 16 == i for c in SCHEDULE) for i in range(len(STAGES) + 1)]
    for code in SCHEDULE:
        stage, k = code // 16, code % 16
        if stage == len(STAGES):
            grad(feats * (1 - k), k == 0)
            continue
        name = STAGES[stage]
        stages[name](k)
        left_of[stage] -= 1
        if left_of[stage] == 0:
            for step in side.get(name, ()):
                step()

    for k in range(nch):
        p13(k)
    ge_v[...] = dot(src[...], dall[...], ((0,), (0,)))
    got1("GB", rpb)
    geb_v[...] = jnp.sum(pb[...] + rpb[0] + rpb[1] + rpb[2], axis=0, keepdims=True)
    gdb_v[...] = jnp.sum(bsum[...], axis=0, keepdims=True)
    got1("L5", rl5)
    layers = 2 * NY
    width = 2 * half
    loss_s[0, 0] = jnp.sum(sl5[...] + rl5[...]) / (2.0 * tok * layers * width)

    own_gd = gd.at[pl.ds(0, feats)]
    pltpu.make_async_copy(own_gd, own_gd, lsem.at[4]).wait()
    got1("GD", own_gd)
    def drain(kind, ref, only=None, skip=()):
        for k in range(nch) if only is None else only:
            if k not in skip:
                r = ref(k)
                pltpu.make_async_copy(r, r, ssem.at[ID[kind]]).wait()

    most = 2 * NY - 1
    drain("YR", lambda k: ry.at[k], skip=PRE_DIRECT)
    drain("ZP", lambda k: zr_p.at[k], skip=PRE_DIRECT)
    drain("D1", lambda k: rd1.at[k, pl.ds(0, most)], only=PRE_DIRECT)
    drain("YB", lambda k: ryb.at[k], skip=BACK_DIRECT)
    drain("ZB", lambda k: zr_b.at[k], skip=BACK_DIRECT)
    drain("D2", lambda k: rd2.at[k, pl.ds(0, most)], only=BACK_DIRECT)
    drain("FP", lambda k: hp.at[span(k)], skip=X_DIRECT)
    drain("FM", lambda k: hm.at[span(k)], skip=X_DIRECT)
    drain("X2", lambda k: eall.at[span(k), pl.ds(0, group)], only=X_DIRECT)
    q3 = 3 * tok // 4
    left = dict(
        YA=acts.at[pl.ds(0, q3), pl.ds(0, feats)], SA=acts.at[:, pl.ds(0, feats)], HP=hp, HM=hm, OP=op, OM=om, AP=ap, AM=am,
        ZR=rz, ZA=eall.at[:, pl.ds(0, 3 * blk)], XP=eall.at[:, pl.ds(0, group)], XM=eall.at[:, pl.ds(0, group)], SB=b_recv,
        YD=dall.at[pl.ds(0, q3)],
    )
    for name, ref in left.items():
        pltpu.make_async_copy(ref, ref, ssem.at[ID[name]]).wait()
    once = dict(W=w.at[pl.ds(0, feats)], GB=rpb, L1=rl1, L2=rl2, L3=rl3, L4=rl4, L5=rl5, GD=own_gd)
    for name, ref in once.items():
        pltpu.make_async_copy(ref, ref, oss.at[OID[name]]).wait()


def place(a, b, c, d, ao, bo, co, do, sem):
    copies = [pltpu.make_async_copy(i, o, sem.at[n]) for n, (i, o) in enumerate(((a, ao), (b, bo), (c, co), (d, do)))]
    for copy in copies:
        copy.start()
    for copy in copies:
        copy.wait()


def shards(source, enc_weight, enc_bias, dec_weight, dec_bias, target):
    tok, depth = source.shape
    feats = enc_weight.shape[1]
    width = dec_weight.shape[2]
    half = width // 2
    group = half // NX
    hg = group // 2
    blk = group // NZ
    nch = tok // CHUNK
    rows = CHUNK // NY
    V = pltpu.VMEM
    any_spec = pl.BlockSpec(memory_space=pl.ANY)
    hbm_spec = pl.BlockSpec(memory_space=pltpu.HBM)
    vmem_spec = pl.BlockSpec(memory_space=pltpu.VMEM)
    scratch = [
        V((tok, depth), BF), V((depth, feats), BF), V((tok, blk), BF), V((1, feats), F32), V((1, blk), F32), V((2 * feats, half), BF),
        V((tok, feats), F32), V((nch, 3, rows, feats), F32), V((nch, rows, feats), F32), V((nch, rows, feats), F32),
        V((nch, rows, feats), F32), V((tok, 2 * feats), BF), V((tok, half), BF), V((tok, group), F32),
        V((tok, hg), BF), V((tok, hg), BF), V((tok, hg), BF), V((tok, hg), BF), V((tok, hg), BF), V((tok, hg), BF),
        V((tok, hg), BF), V((tok, hg), BF), V((tok, group), BF), V((tok, blk), F32), V((nch, 3, CHUNK, blk), BF), V((tok, half), BF),
        V((tok, feats), F32), V((tok, feats), F32), V((tok, feats), F32), V((tok, feats), BF), V((nch, 3, rows, feats), BF),
        V((nch, rows, feats), F32), V((nch, rows, feats), F32), V((tok, feats), BF), V((2 * feats, half), BF),
        V((8, feats), F32), V((3, 8, feats), F32), V((8, blk), F32), V((3, 8, blk), F32), V((3, 8, blk), F32), V((8, blk), F32),
        V((3, 8, blk), F32), V((8, blk), F32), V((8, blk), F32), V((8, blk), F32), V((8, blk), F32), V((8, blk), F32), V((8, blk), F32),
        V((tok, feats), BF), V((nch, 2 * NY, rows, feats), BF), V((nch, 2 * NY, rows, feats), BF),
        pltpu.SemaphoreType.DMA((7,)), pltpu.SemaphoreType.DMA((len(KINDS),)), pltpu.SemaphoreType.DMA((len(KINDS), nch)),
        pltpu.SemaphoreType.DMA((len(ONCE),)), pltpu.SemaphoreType.DMA((len(ONCE),)),
    ]
    ge, geb, gd, gdb, loss = pl.pallas_call(
        kernel,
        out_shape=(
            jax.ShapeDtypeStruct((depth, feats), F32),
            jax.ShapeDtypeStruct((1, feats), F32),
            jax.ShapeDtypeStruct((1, feats, width), BF),
            jax.ShapeDtypeStruct((1, blk), F32),
            jax.ShapeDtypeStruct((1, 1), F32),
        ),
        in_specs=[any_spec] * 6,
        out_specs=(vmem_spec, vmem_spec, any_spec, vmem_spec, pl.BlockSpec(memory_space=pltpu.SMEM)),
        scratch_shapes=scratch,
        compiler_params=pltpu.CompilerParams(collective_id=0, has_side_effects=True, vmem_limit_bytes=45 << 20),
    )(*(pltpu.with_memory_space_constraint(v, pltpu.HBM) for v in (source, enc_weight, enc_bias.reshape(1, feats), dec_weight, dec_bias, target)))
    outs = (ge, geb, gd, gdb)
    ge, geb, gd, gdb = pl.pallas_call(
        place,
        out_shape=tuple(pltpu.HBM(v.shape, v.dtype) for v in outs),
        in_specs=[any_spec] * 4,
        out_specs=(any_spec,) * 4,
        scratch_shapes=[pltpu.SemaphoreType.DMA((4,))],
        compiler_params=pltpu.CompilerParams(vmem_limit_bytes=1 << 20),
    )(*(pltpu.with_memory_space_constraint(v, pltpu.VMEM) for v in outs))
    return ge, geb.reshape(feats), gd, gdb, loss.reshape(())


def solution(mesh):
    return jax.shard_map(
        shards,
        mesh=mesh,
        in_specs=(
            P(None, "layer"),
            P("layer", "feat"),
            P("feat"),
            P("layer", "feat", None),
            P("layer", None),
            P("layer", None, None),
        ),
        out_specs=(
            P("layer", "feat"),
            P("feat"),
            P("layer", "feat", None),
            P("layer", "feat"),
            P(),
        ),
        check_vma=False,
    )
```

```python
import functools

import jax
import jax.numpy as jnp
from jax import lax
from jax.experimental import pallas as pl
from jax.experimental.pallas import tpu as pltpu
from jax.sharding import PartitionSpec as P

BF = jnp.bfloat16
F32 = jnp.float32
MESH = pl.DeviceIdType.MESH

NY, NX, NZ = 4, 4, 4
CHUNK = 64
STAGES = ("P1", "P2", "P3", "P4", "P5", "P6A", "P6", "P7", "P8", "P8A", "P9", "P10", "P11", "P12")
SCHEDULE = (
    6, 0, 5, 3, 22, 1, 21, 32, 38, 19, 37, 4, 48, 17, 54, 7, 35, 64, 2, 53,
    70, 20, 69, 80, 51, 33, 23, 86, 36, 18, 67, 96, 49, 85, 34, 102, 52, 83, 39, 65,
    101, 68, 112, 50, 55, 81, 99, 66, 118, 71, 117, 84, 97, 82, 128, 115, 100, 134, 87, 98,
    133, 113, 144, 103, 150, 131, 116, 160, 149, 114, 129, 166, 119, 147, 176, 132, 165, 182, 145, 130,
    192, 135, 181, 163, 198, 148, 161, 146, 208, 179, 151, 177, 197, 164, 214, 162, 180, 167, 195, 178,
    193, 183, 224, 196, 213, 211, 194, 209, 215, 212, 210, 225,
)
PRE_DIRECT, BACK_DIRECT, X_DIRECT = (0,), (7,), ()
KINDS = ("YR", "ZP", "YA", "SA", "HP", "HM", "OP", "OM", "AP", "AM", "ZR", "ZA", "XP", "XM", "FP", "FM", "SB", "YB", "ZB", "YD", "D1", "D2", "X2")
ID = {name: i for i, name in enumerate(KINDS)}
ONCE = ("W", "GB", "L1", "L2", "L3", "L4", "L5", "GD")
OID = {name: i for i, name in enumerate(ONCE)}
A0 = 0.7978845608
A1 = 0.044715


def dot(a, b, dims):
    return lax.dot_general(a, b, (dims, ((), ())), preferred_element_type=F32)


def kernel(
    src_h, enc_h, encb_h, w_h, decb_h, tgt_h,
    ge_v, geb_v, gd_h, gdb_v, loss_s,
    src, enc, tgt, encb_v, decb_v, w, ps, ry, zs_p, zr_p, gpr, acts, rec, own, hp, hm, op, om, ap, am, sp, sm, zsend, zown, rz, eall,
    b_own, b_send, b_recv, by, ryb, zs_b, zr_b, dall, gd, pb, rpb, sq, rl1, rl2, rl3, rl4, rl5, sl2, sl3, sl4, sl5, bsum, psb, rd1, rd2, wt,
    lsem, ssem, rsem, oss, ors,
):
    tok, depth = src.shape
    feats = enc.shape[1]
    half = w.shape[1]
    tt = CHUNK
    nch = tok // tt
    rows = tt // NY
    group = half // NX
    hg = group // 2
    blk = group // NZ
    lay, fea = lax.axis_index("layer"), lax.axis_index("feat")
    zl, y = lay // NY, lay % NY
    zh, x, core = fea // (2 * NX), (fea // 2) % NX, fea % 2

    def dev(dzl=0, dy=0, dzh=0, dx=0, dc=0):
        return (
            ((zl + dzl) % 2) * NY + (y + dy) % NY,
            ((zh + dzh) % NZ) * (2 * NX) + ((x + dx) % NX) * 2 + (core + dc) % 2,
        )

    def send(kind, k, src_ref, dst_ref, to):
        pltpu.make_async_remote_copy(
            src_ref, dst_ref, ssem.at[ID[kind]], rsem.at[ID[kind], k], device_id=to, device_id_type=MESH
        ).start()

    def got(kind, k, ref):
        pltpu.make_async_copy(ref, ref, rsem.at[ID[kind], k]).wait()

    def send1(kind, src_ref, dst_ref, to):
        pltpu.make_async_remote_copy(
            src_ref, dst_ref, oss.at[OID[kind]], ors.at[OID[kind]], device_id=to, device_id_type=MESH
        ).start()

    def got1(kind, ref):
        pltpu.make_async_copy(ref, ref, ors.at[OID[kind]]).wait()

    barrier = pltpu.get_barrier_semaphore()
    peers = (
        [dict(dzl=z, dy=o) for z in range(2) for o in range(NY) if z or o] + [dict(dc=1)]
        + [dict(dx=o) for o in range(1, NX)] + [dict(dzh=o) for o in range(1, NZ)]
    )
    for p in peers:
        pl.semaphore_signal(barrier, inc=1, device_id=dev(**p), device_id_type=MESH)

    c_src = pltpu.make_async_copy(src_h, src, lsem.at[0])
    c_enc = pltpu.make_async_copy(enc_h, enc, lsem.at[1])
    c_src.start()
    c_enc.start()

    def column(o, p, c):
        return pl.multiple_of((((zh + p) % NZ) * (2 * NX) + ((x + o) % NX) * 2 + c) * blk, blk)

    for o in range(NX):
        for p in range(NZ):
            pltpu.make_async_copy(
                w_h.at[0, :, pl.ds(column(o, p, core), blk)],
                w.at[pl.ds(0, feats), pl.ds((o * NZ + p) * blk, blk)],
                lsem.at[2],
            ).start()
    c_tgt = pltpu.make_async_copy(tgt_h.at[0, :, pl.ds(pl.multiple_of(fea * blk, blk), blk)], tgt, lsem.at[3])
    c_tgt.start()
    c_encb = pltpu.make_async_copy(encb_h, encb_v, lsem.at[5])
    c_encb.start()
    c_decb = pltpu.make_async_copy(decb_h.at[:, pl.ds(pl.multiple_of(fea * blk, blk), blk)], decb_v, lsem.at[6])
    c_decb.start()
    c_src.wait()
    c_enc.wait()
    c_encb.wait()
    ps[...] = dot(src[...], enc[...], ((1,), (0,)))
    for k in PRE_DIRECT:
        psb[pl.ds(k * tt, tt)] = ps[pl.ds(k * tt, tt)].astype(BF)
    pl.semaphore_wait(barrier, len(peers))
    sq[...] = jnp.zeros_like(sq)
    pb[...] = jnp.zeros_like(pb)
    bsum[...] = jnp.zeros_like(bsum)

    def swap():
        for o in range(NX):
            for p in range(NZ):
                send1(
                    "W", w_h.at[0, :, pl.ds(column(o, p, 1 - core), blk)],
                    w.at[pl.ds(feats, feats), pl.ds((o * NZ + p) * blk, blk)], dev(dc=1),
                )

    last_p9 = [c % 16 for c in SCHEDULE if c // 16 == STAGES.index("P9")][-1]
    last_p12 = [c % 16 for c in SCHEDULE if c // 16 == STAGES.index("P12")][-1]
    b_send[pl.ds(last_p9 * tt, tt)] = jnp.zeros((tt, feats), F32)
    b_own[pl.ds(last_p9 * tt, tt)] = jnp.zeros((tt, feats), F32)

    def span(k):
        return pl.ds(k * tt, tt)

    def piece(k, yy):
        return pl.ds(pl.multiple_of(k * tt + yy * rows, rows), rows)

    def fold(v):
        return jnp.sum(v.reshape(v.shape[0] // 8, 8, v.shape[1]), axis=0)

    def everyone(kind, k, buf, slots):
        slots[lay] = buf[piece(k, y)]
        for dzl in range(2):
            for o in range(NY):
                if dzl or o:
                    send(kind, k, buf.at[piece(k, (y + o) % NY)], slots.at[lay], dev(dzl=dzl, dy=o))

    def total(slots):
        v = slots[0].astype(F32)
        for i in range(1, 2 * NY):
            v = v + slots[i].astype(F32)
        return v

    def p1(k):
        if k in PRE_DIRECT:
            everyone("D1", k, psb, rd1.at[k])
            return
        for o in range(1, NY):
            send("YR", k, ps.at[piece(k, (y + o) % NY)], ry.at[k, o - 1], dev(dy=o))

    def p2(k):
        got("YR", k, ry.at[k])
        zs_p[k] = ps[piece(k, y)] + ry[k, 0] + ry[k, 1] + ry[k, 2]
        send("ZP", k, zs_p.at[k], zr_p.at[k], dev(dzl=1))

    def p3(k):
        if k in PRE_DIRECT:
            got("D1", k, rd1.at[k, pl.ds(0, 2 * NY - 1)])
            v = total(rd1.at[k]) + encb_v[...]
        else:
            got("ZP", k, zr_p.at[k])
            v = zs_p[k] + zr_p[k] + encb_v[...]
        v2 = v * v
        t = jnp.tanh(A0 * (v * (1.0 + A1 * v2)))
        h = 0.5 * (1.0 + t)
        acts[piece(k, y), pl.ds(0, feats)] = (v * h).astype(BF)
        for o in range(1, NY):
            r = acts.at[piece(k, y), pl.ds(0, feats)]
            send("YA", k, r, r, dev(dy=o))
        gpr[k] = h + 0.5 * v * (1.0 - t * t) * (A0 * (1.0 + 3.0 * A1 * v2))

    def p4(k):
        got("YA", k, acts.at[pl.ds(0, 3 * rows), pl.ds(0, feats)])
        send("SA", k, acts.at[span(k), pl.ds(0, feats)], acts.at[span(k), pl.ds(feats, feats)], dev(dc=1))

    def p5(k):
        got("SA", k, acts.at[span(k), pl.ds(feats, feats)])

        if k == 0:
            pltpu.make_async_copy(w.at[pl.ds(0, feats)], w.at[pl.ds(0, feats)], lsem.at[2]).wait()
            got1("W", w.at[pl.ds(feats, feats)])

        a = acts[span(k)]
        s = span(k)
        for o in (2, 1, 3):
            rec[s, pl.ds(o * group, group)] = dot(a, w[:, pl.ds(o * group, group)], ((1,), (0,))).astype(BF)
            if o == 2:
                send("HP", k, rec.at[s, pl.ds(2 * group, hg)], hp.at[s], dev(dx=1))
                send("HM", k, rec.at[s, pl.ds(2 * group + hg, hg)], hm.at[s], dev(dx=3))
            elif o == 1:
                send("OP", k, rec.at[s, pl.ds(group + hg, hg)], op.at[s], dev(dx=1))
            else:
                send("OM", k, rec.at[s, pl.ds(3 * group, hg)], om.at[s], dev(dx=3))
        own[s] = dot(a, w[:, pl.ds(0, group)], ((1,), (0,)))

    def p6a(k):
        s = span(k)
        got("HP", k, hp.at[s])
        sp[s] = (hp[s].astype(F32) + rec[s, pl.ds(group, hg)].astype(F32)).astype(BF)
        send("AP", k, sp.at[s], ap.at[s], dev(dx=1))
        got("HM", k, hm.at[s])
        sm[s] = (hm[s].astype(F32) + rec[s, pl.ds(3 * group + hg, hg)].astype(F32)).astype(BF)
        send("AM", k, sm.at[s], am.at[s], dev(dx=3))

    def p6(k):
        s = span(k)
        got("OP", k, op.at[s])
        got("OM", k, om.at[s])
        got("AP", k, ap.at[s])
        got("AM", k, am.at[s])
        first = own[s, pl.ds(0, hg)] + ap[s].astype(F32) + om[s].astype(F32)
        second = own[s, pl.ds(hg, hg)] + am[s].astype(F32) + op[s].astype(F32)
        zown[s] = first[:, :blk]
        zsend[s, pl.ds(0, hg)] = first.astype(BF)
        zsend[s, pl.ds(hg, hg)] = second.astype(BF)
        for p in range(1, NZ):
            send("ZR", k, zsend.at[s, pl.ds(p * blk, blk)], rz.at[k, p - 1], dev(dzh=p))

    def p7(k):
        s = span(k)
        got("ZR", k, rz.at[k])
        recon = zown[s] + rz[k, 0].astype(F32) + rz[k, 1].astype(F32) + rz[k, 2].astype(F32)

        if k == 0:
            c_tgt.wait()
            c_decb.wait()

        err = recon + decb_v[...] - tgt[s].astype(F32)
        eall[s, pl.ds(0, blk)] = err.astype(BF)
        for p in range(1, NZ):
            send("ZA", k, eall.at[s, pl.ds(0, blk)], eall.at[s, pl.ds((NZ - p) * blk, blk)], dev(dzh=p))
        bsum[...] += fold(err)
        sq[...] += fold(err * err)

    def p8(k):
        s = span(k)
        got("ZA", k, eall.at[s, pl.ds(blk, 3 * blk)])
        send("XP", k, eall.at[s, pl.ds(0, group)], eall.at[s, pl.ds(3 * group, group)], dev(dx=1))
        send("XM", k, eall.at[s, pl.ds(0, group)], eall.at[s, pl.ds(group, group)], dev(dx=3))
        if k in X_DIRECT:
            send("X2", k, eall.at[s, pl.ds(0, group)], eall.at[s, pl.ds(2 * group, group)], dev(dx=2))

    def p8a(k):
        s = span(k)
        got("XP", k, eall.at[s, pl.ds(3 * group, group)])
        send("FP", k, eall.at[s, pl.ds(3 * group, hg)], eall.at[s, pl.ds(2 * group, hg)], dev(dx=1))
        got("XM", k, eall.at[s, pl.ds(group, group)])
        send("FM", k, eall.at[s, pl.ds(group + hg, hg)], eall.at[s, pl.ds(2 * group + hg, hg)], dev(dx=3))

    def p9(k):
        s = span(k)
        late = k == last_p9
        if k in X_DIRECT:
            got("XP", k, eall.at[s, pl.ds(3 * group, group)])
            got("XM", k, eall.at[s, pl.ds(group, group)])
        if late:
            for c in (pl.ds(0, 2 * group), pl.ds(3 * group, group)):
                b_send[s] += dot(eall[s, c], wt[c, pl.ds(feats, feats)], ((1,), (0,)))
                b_own[s] += dot(eall[s, c], wt[c, pl.ds(0, feats)], ((1,), (0,)))
        if k in X_DIRECT:
            got("X2", k, eall.at[s, pl.ds(2 * group, group)])
        else:
            got("FP", k, eall.at[s, pl.ds(2 * group, hg)])
            got("FM", k, eall.at[s, pl.ds(2 * group + hg, hg)])
        if late:
            c = pl.ds(2 * group, group)
            b_send[s] += dot(eall[s, c], wt[c, pl.ds(feats, feats)], ((1,), (0,)))
            send("SB", k, b_send.at[s], b_recv.at[s], dev(dc=1))
            b_own[s] += dot(eall[s, c], wt[c, pl.ds(0, feats)], ((1,), (0,)))
        else:
            e = eall[s]
            b_send[s] = dot(e, wt[:, pl.ds(feats, feats)], ((1,), (0,)))
            send("SB", k, b_send.at[s], b_recv.at[s], dev(dc=1))
            b_own[s] = dot(e, wt[:, pl.ds(0, feats)], ((1,), (0,)))

    def p10(k):
        s = span(k)
        got("SB", k, b_recv.at[s])
        by[s] = (b_own[s] + b_recv[s]).astype(BF)
        if k in BACK_DIRECT:
            everyone("D2", k, by, rd2.at[k])
            return
        for o in range(1, NY):
            send("YB", k, by.at[piece(k, (y + o) % NY)], ryb.at[k, o - 1], dev(dy=o))

    def p11(k):
        got("YB", k, ryb.at[k])
        me = piece(k, y)
        zs_b[k] = (
            b_own[me] + b_recv[me] + ryb[k, 0].astype(F32) + ryb[k, 1].astype(F32) + ryb[k, 2].astype(F32)
        )
        send("ZB", k, zs_b.at[k], zr_b.at[k], dev(dzl=1))

    def p12(k):
        if k in BACK_DIRECT:
            got("D2", k, rd2.at[k, pl.ds(0, 2 * NY - 1)])
            dpre = total(rd2.at[k]) * gpr[k]
        else:
            got("ZB", k, zr_b.at[k])
            dpre = (zs_b[k] + zr_b[k]) * gpr[k]
        r = dall.at[piece(k, y)]
        dall[piece(k, y)] = dpre.astype(BF)
        for o in range(1, NY):
            send("YD", k, r, r, dev(dy=o))
        pb[...] += fold(dpre)


    def p13(k):
        got("YD", k, dall.at[pl.ds(0, 3 * rows)])

    stages = dict(P1=p1, P2=p2, P3=p3, P4=p4, P5=p5, P6A=p6a, P6=p6, P7=p7, P8=p8, P8A=p8a, P9=p9, P10=p10, P11=p11, P12=p12)

    def grad(base, which):
        def body(n, _):
            at = pl.multiple_of(n * group, group)
            gd[pl.ds(base, feats), pl.ds(at, group)] = dot(
                acts[:, pl.ds(base, feats)], eall[:, pl.ds(at, group)], ((0,), (0,))
            ).astype(BF)
            for p in range(NZ):
                part = gd.at[pl.ds(base, feats), pl.ds(pl.multiple_of(at + p * blk, blk), blk)]
                where = gd_h.at[0, :, pl.ds(column(n, p, core), blk)]
                if which:
                    send1("GD", part, where, dev(dc=1))
                else:
                    pltpu.make_async_copy(part, where, lsem.at[4]).start()
            return 0

        lax.fori_loop(0, NX, body, 0)

    def bias():
        for o in range(1, NY):
            send1("GB", pb, rpb.at[o - 1], dev(dy=o))

    def l1():
        for o in range(1, NZ):
            send1("L1", sq, rl1.at[o - 1], dev(dzh=o))

    def l2():
        got1("L1", rl1)
        sl2[...] = sq[...] + rl1[0] + rl1[1] + rl1[2]
        for o in range(1, NX):
            send1("L2", sl2, rl2.at[o - 1], dev(dx=o))

    def l3():
        got1("L2", rl2)
        sl3[...] = sl2[...] + rl2[0] + rl2[1] + rl2[2]
        send1("L3", sl3, rl3, dev(dc=1))

    def l4():
        got1("L3", rl3)
        sl4[...] = sl3[...] + rl3[...]
        for o in range(1, NY):
            send1("L4", sl4, rl4.at[o - 1], dev(dy=o))

    def l5():
        got1("L4", rl4)
        sl5[...] = sl4[...] + rl4[0] + rl4[1] + rl4[2]
        send1("L5", sl5, rl5, dev(dzl=1))

    side = {"P7": (l1,), "P8": (l2,), "P9": (l3,), "P10": (l4,), "P12": (bias, l5)}
    left_of = [sum(c // 16 == i for c in SCHEDULE) for i in range(len(STAGES) + 1)]
    for at, code in enumerate(SCHEDULE):
        if at == 0:
            swap()
        stage, k = code // 16, code % 16
        if stage == len(STAGES):
            grad(feats * (1 - k), k == 0)
            continue
        name = STAGES[stage]
        stages[name](k)
        seen = left_of[4]
        left_of[stage] -= 1
        if name == "P5" and nch - NX - 1 < seen <= nch - 1:
            q = pl.ds((nch - 1 - seen) * group, group)
            wt[q, :] = w[:, q].T
        if left_of[stage] == 0:
            for step in side.get(name, ()):
                step()

    gdb_v[...] = jnp.sum(bsum[...], axis=0, keepdims=True)
    for k in range(nch):
        if k != last_p12:
            p13(k)

    def drain(kind, ref, only=None, skip=()):
        for k in range(nch) if only is None else only:
            if k not in skip:
                r = ref(k)
                pltpu.make_async_copy(r, r, ssem.at[ID[kind]]).wait()

    most = 2 * NY - 1
    drain("YR", lambda k: ry.at[k], skip=PRE_DIRECT)
    drain("ZP", lambda k: zr_p.at[k], skip=PRE_DIRECT)
    drain("D1", lambda k: rd1.at[k, pl.ds(0, most)], only=PRE_DIRECT)
    drain("YB", lambda k: ryb.at[k], skip=BACK_DIRECT)
    drain("ZB", lambda k: zr_b.at[k], skip=BACK_DIRECT)
    drain("D2", lambda k: rd2.at[k, pl.ds(0, most)], only=BACK_DIRECT)
    drain("FP", lambda k: hp.at[span(k)], skip=X_DIRECT)
    drain("FM", lambda k: hm.at[span(k)], skip=X_DIRECT)
    drain("X2", lambda k: eall.at[span(k), pl.ds(0, group)], only=X_DIRECT)
    q3 = 3 * tok // 4
    left = dict(
        YA=acts.at[pl.ds(0, q3), pl.ds(0, feats)], SA=acts.at[:, pl.ds(0, feats)], HP=hp, HM=hm, OP=op, OM=om, AP=ap, AM=am,
        ZR=rz, ZA=eall.at[:, pl.ds(0, 3 * blk)], XP=eall.at[:, pl.ds(0, group)], XM=eall.at[:, pl.ds(0, group)], SB=b_recv,
    )
    for name, ref in left.items():
        pltpu.make_async_copy(ref, ref, ssem.at[ID[name]]).wait()
    once = dict(W=w.at[pl.ds(0, feats)], L1=rl1, L2=rl2, L3=rl3, L4=rl4)
    for name, ref in once.items():
        pltpu.make_async_copy(ref, ref, oss.at[OID[name]]).wait()
    own_gd = gd.at[pl.ds(0, feats)]
    pltpu.make_async_copy(own_gd, own_gd, lsem.at[4]).wait()
    got1("L5", rl5)
    loss_s[0, 0] = jnp.sum(sl5[...] + rl5[...]) / (2.0 * tok * (2 * NY) * (2 * half))

    p13(last_p12)
    ge_v[...] = dot(src[...], dall[...], ((0,), (0,)))
    got1("GB", rpb)
    geb_v[...] = jnp.sum(pb[...] + rpb[0] + rpb[1] + rpb[2], axis=0, keepdims=True)
    got1("GD", own_gd)
    r = dall.at[pl.ds(0, q3)]
    pltpu.make_async_copy(r, r, ssem.at[ID["YD"]]).wait()
    for name, ref in dict(GB=rpb, L5=rl5, GD=own_gd).items():
        pltpu.make_async_copy(ref, ref, oss.at[OID[name]]).wait()


def place(a, b, c, d, ao, bo, co, do, sem):
    parts = [(b, bo), (d, do)]
    for i in range(4):
        r = pl.ds(i * (c.shape[1] // 4), c.shape[1] // 4)
        parts.append((c.at[:, r], co.at[:, r]))
    for i in range(2):
        r = pl.ds(i * (a.shape[0] // 2), a.shape[0] // 2)
        parts.append((a.at[r], ao.at[r]))
    copies = [pltpu.make_async_copy(i, o, sem.at[n]) for n, (i, o) in enumerate(parts)]
    for copy in copies:
        copy.start()
    for copy in copies:
        copy.wait()


def shards(source, enc_weight, enc_bias, dec_weight, dec_bias, target):
    tok, depth = source.shape
    feats = enc_weight.shape[1]
    width = dec_weight.shape[2]
    half = width // 2
    group = half // NX
    hg = group // 2
    blk = group // NZ
    nch = tok // CHUNK
    rows = CHUNK // NY
    V = pltpu.VMEM
    any_spec = pl.BlockSpec(memory_space=pl.ANY)
    hbm_spec = pl.BlockSpec(memory_space=pltpu.HBM)
    vmem_spec = pl.BlockSpec(memory_space=pltpu.VMEM)
    scratch = [
        V((tok, depth), BF), V((depth, feats), BF), V((tok, blk), BF), V((1, feats), F32), V((1, blk), F32), V((2 * feats, half), BF),
        V((tok, feats), F32), V((nch, 3, rows, feats), F32), V((nch, rows, feats), F32), V((nch, rows, feats), F32),
        V((nch, rows, feats), F32), V((tok, 2 * feats), BF), V((tok, half), BF), V((tok, group), F32),
        V((tok, hg), BF), V((tok, hg), BF), V((tok, hg), BF), V((tok, hg), BF), V((tok, hg), BF), V((tok, hg), BF),
        V((tok, hg), BF), V((tok, hg), BF), V((tok, group), BF), V((tok, blk), F32), V((nch, 3, CHUNK, blk), BF), V((tok, half), BF),
        V((tok, feats), F32), V((tok, feats), F32), V((tok, feats), F32), V((tok, feats), BF), V((nch, 3, rows, feats), BF),
        V((nch, rows, feats), F32), V((nch, rows, feats), F32), V((tok, feats), BF), V((2 * feats, half), BF),
        V((8, feats), F32), V((3, 8, feats), F32), V((8, blk), F32), V((3, 8, blk), F32), V((3, 8, blk), F32), V((8, blk), F32),
        V((3, 8, blk), F32), V((8, blk), F32), V((8, blk), F32), V((8, blk), F32), V((8, blk), F32), V((8, blk), F32), V((8, blk), F32),
        V((tok, feats), BF), V((nch, 2 * NY, rows, feats), BF), V((nch, 2 * NY, rows, feats), BF), V((half, 2 * feats), BF),
        pltpu.SemaphoreType.DMA((7,)), pltpu.SemaphoreType.DMA((len(KINDS),)), pltpu.SemaphoreType.DMA((len(KINDS), nch)),
        pltpu.SemaphoreType.DMA((len(ONCE),)), pltpu.SemaphoreType.DMA((len(ONCE),)),
    ]
    ge, geb, gd, gdb, loss = pl.pallas_call(
        kernel,
        out_shape=(
            jax.ShapeDtypeStruct((depth, feats), F32),
            jax.ShapeDtypeStruct((1, feats), F32),
            jax.ShapeDtypeStruct((1, feats, width), BF),
            jax.ShapeDtypeStruct((1, blk), F32),
            jax.ShapeDtypeStruct((1, 1), F32),
        ),
        in_specs=[any_spec] * 6,
        out_specs=(vmem_spec, vmem_spec, any_spec, vmem_spec, pl.BlockSpec(memory_space=pltpu.SMEM)),
        scratch_shapes=scratch,
        compiler_params=pltpu.CompilerParams(collective_id=0, has_side_effects=True, vmem_limit_bytes=45 << 20),
    )(*(pltpu.with_memory_space_constraint(v, pltpu.HBM) for v in (source, enc_weight, enc_bias.reshape(1, feats), dec_weight, dec_bias, target)))
    outs = (ge, geb, gd, gdb)
    ge, geb, gd, gdb = pl.pallas_call(
        place,
        out_shape=tuple(pltpu.HBM(v.shape, v.dtype) for v in outs),
        in_specs=[any_spec] * 4,
        out_specs=(any_spec,) * 4,
        scratch_shapes=[pltpu.SemaphoreType.DMA((8,))],
        compiler_params=pltpu.CompilerParams(vmem_limit_bytes=1 << 20),
    )(*(pltpu.with_memory_space_constraint(v, pltpu.VMEM) for v in outs))
    return ge, geb.reshape(feats), gd, gdb, loss.reshape(())


def solution(mesh):
    return jax.shard_map(
        shards,
        mesh=mesh,
        in_specs=(
            P(None, "layer"),
            P("layer", "feat"),
            P("feat"),
            P("layer", "feat", None),
            P("layer", None),
            P("layer", None, None),
        ),
        out_specs=(
            P("layer", "feat"),
            P("feat"),
            P("layer", "feat", None),
            P("layer", "feat"),
            P(),
        ),
        check_vma=False,
    )
```

```python
import functools

import jax
import jax.numpy as jnp
from jax import lax
from jax.experimental import pallas as pl
from jax.experimental.pallas import tpu as pltpu
from jax.sharding import PartitionSpec as P

BF = jnp.bfloat16
F32 = jnp.float32
MESH = pl.DeviceIdType.MESH

NY, NX, NZ = 4, 4, 4
FAR_FIRST = (2, 1, 3)
CHUNK = 64
STAGES = ("P1", "P2", "P3", "P4", "P5", "P6A", "P6", "P7", "P8", "P8A", "P9", "P10", "P11", "P12")
SCHEDULE = (
    6, 0, 5, 3, 22, 1, 21, 32, 38, 19, 37, 4, 48, 17, 54, 7, 35, 64, 2, 53,
    70, 20, 69, 80, 51, 33, 23, 86, 36, 18, 67, 96, 49, 85, 34, 102, 52, 83, 39, 65,
    101, 68, 112, 50, 55, 81, 99, 66, 118, 71, 117, 84, 97, 82, 128, 115, 100, 134, 87, 98,
    133, 113, 144, 103, 150, 131, 116, 160, 149, 114, 129, 166, 119, 147, 176, 132, 165, 182, 145, 130,
    192, 135, 181, 163, 198, 148, 161, 146, 208, 179, 151, 177, 197, 164, 214, 162, 180, 167, 195, 178,
    193, 183, 224, 196, 213, 211, 194, 209, 215, 212, 210, 225,
)
PRE_DIRECT, BACK_DIRECT, X_DIRECT = (0,), (7,), ()
KINDS = ("YR", "ZP", "YA", "SA", "HP", "HM", "OP", "OM", "AP", "AM", "ZR", "ZA", "XP", "XM", "FP", "FM", "SB", "YB", "ZB", "YD", "D1", "D2", "X2")
ID = {name: i for i, name in enumerate(KINDS)}
ONCE = ("W", "GB", "L1", "L2", "L3", "L4", "L5", "GD")
OID = {name: i for i, name in enumerate(ONCE)}
A0 = 0.7978845608
A1 = 0.044715


def dot(a, b, dims):
    return lax.dot_general(a, b, (dims, ((), ())), preferred_element_type=F32)


def kernel(
    src_h, enc_h, encb_h, w_h, decb_h, tgt_h,
    ge_v, geb_v, gd_h, gdb_v, loss_s,
    src, enc, tgt, encb_v, decb_v, w, ps, ry, zs_p, zr_p, gpr, acts, rec, own, hp, hm, op, om, ap, am, sp, sm, zsend, zown, rz, eall,
    b_own, b_send, b_recv, by, ryb, zs_b, zr_b, dall, gd, pb, rpb, sq, rl1, rl2, rl3, rl4, rl5, sl2, sl3, sl4, sl5, bsum, psb, rd1, rd2, wt,
    lsem, ssem, rsem, oss, ors,
):
    tok, depth = src.shape
    feats = enc.shape[1]
    half = w.shape[1]
    tt = CHUNK
    nch = tok // tt
    rows = tt // NY
    group = half // NX
    hg = group // 2
    blk = group // NZ
    lay, fea = lax.axis_index("layer"), lax.axis_index("feat")
    zl, y = lay // NY, lay % NY
    zh, x, core = fea // (2 * NX), (fea // 2) % NX, fea % 2

    def dev(dzl=0, dy=0, dzh=0, dx=0, dc=0):
        return (
            ((zl + dzl) % 2) * NY + (y + dy) % NY,
            ((zh + dzh) % NZ) * (2 * NX) + ((x + dx) % NX) * 2 + (core + dc) % 2,
        )

    def send(kind, k, src_ref, dst_ref, to):
        pltpu.make_async_remote_copy(
            src_ref, dst_ref, ssem.at[ID[kind]], rsem.at[ID[kind], k], device_id=to, device_id_type=MESH
        ).start()

    def got(kind, k, ref):
        pltpu.make_async_copy(ref, ref, rsem.at[ID[kind], k]).wait()

    def send1(kind, src_ref, dst_ref, to):
        pltpu.make_async_remote_copy(
            src_ref, dst_ref, oss.at[OID[kind]], ors.at[OID[kind]], device_id=to, device_id_type=MESH
        ).start()

    def got1(kind, ref):
        pltpu.make_async_copy(ref, ref, ors.at[OID[kind]]).wait()

    barrier = pltpu.get_barrier_semaphore()
    peers = (
        [dict(dzl=z, dy=o) for z in range(2) for o in range(NY) if z or o] + [dict(dc=1)]
        + [dict(dx=o) for o in range(1, NX)] + [dict(dzh=o) for o in range(1, NZ)]
    )
    for p in peers:
        pl.semaphore_signal(barrier, inc=1, device_id=dev(**p), device_id_type=MESH)

    c_src = pltpu.make_async_copy(src_h, src, lsem.at[0])
    c_enc = pltpu.make_async_copy(enc_h, enc, lsem.at[1])
    c_src.start()
    c_enc.start()

    def column(o, p, c):
        return pl.multiple_of((((zh + p) % NZ) * (2 * NX) + ((x + o) % NX) * 2 + c) * blk, blk)

    for o in range(NX):
        for p in range(NZ):
            pltpu.make_async_copy(
                w_h.at[0, :, pl.ds(column(o, p, core), blk)],
                w.at[pl.ds(0, feats), pl.ds((o * NZ + p) * blk, blk)],
                lsem.at[2],
            ).start()
    c_tgt = pltpu.make_async_copy(tgt_h.at[0, :, pl.ds(pl.multiple_of(fea * blk, blk), blk)], tgt, lsem.at[3])
    c_tgt.start()
    c_encb = pltpu.make_async_copy(encb_h, encb_v, lsem.at[5])
    c_encb.start()
    c_decb = pltpu.make_async_copy(decb_h.at[:, pl.ds(pl.multiple_of(fea * blk, blk), blk)], decb_v, lsem.at[6])
    c_decb.start()
    c_src.wait()
    c_enc.wait()
    c_encb.wait()
    ps[...] = dot(src[...], enc[...], ((1,), (0,)))
    for k in PRE_DIRECT:
        psb[pl.ds(k * tt, tt)] = ps[pl.ds(k * tt, tt)].astype(BF)
    pl.semaphore_wait(barrier, len(peers))
    sq[...] = jnp.zeros_like(sq)
    pb[...] = jnp.zeros_like(pb)
    bsum[...] = jnp.zeros_like(bsum)

    def swap():
        for o in range(NX):
            for p in range(NZ):
                send1(
                    "W", w_h.at[0, :, pl.ds(column(o, p, 1 - core), blk)],
                    w.at[pl.ds(feats, feats), pl.ds((o * NZ + p) * blk, blk)], dev(dc=1),
                )

    last_p9 = [c % 16 for c in SCHEDULE if c // 16 == STAGES.index("P9")][-1]
    last_p12 = [c % 16 for c in SCHEDULE if c // 16 == STAGES.index("P12")][-1]
    b_send[pl.ds(last_p9 * tt, tt)] = jnp.zeros((tt, feats), F32)
    b_own[pl.ds(last_p9 * tt, tt)] = jnp.zeros((tt, feats), F32)

    def span(k):
        return pl.ds(k * tt, tt)

    def piece(k, yy):
        return pl.ds(pl.multiple_of(k * tt + yy * rows, rows), rows)

    def fold(v):
        return jnp.sum(v.reshape(v.shape[0] // 8, 8, v.shape[1]), axis=0)

    def everyone(kind, k, buf, slots):
        slots[lay] = buf[piece(k, y)]
        for dzl, o in ((1, 2), (0, 2), (1, 1), (1, 3), (0, 1), (0, 3), (1, 0)):
            send(kind, k, buf.at[piece(k, (y + o) % NY)], slots.at[lay], dev(dzl=dzl, dy=o))

    def total(slots):
        v = slots[0].astype(F32)
        for i in range(1, 2 * NY):
            v = v + slots[i].astype(F32)
        return v

    def p1(k):
        if k in PRE_DIRECT:
            everyone("D1", k, psb, rd1.at[k])
            return
        for o in FAR_FIRST:
            send("YR", k, ps.at[piece(k, (y + o) % NY)], ry.at[k, o - 1], dev(dy=o))

    def p2(k):
        got("YR", k, ry.at[k])
        zs_p[k] = ps[piece(k, y)] + ry[k, 0] + ry[k, 1] + ry[k, 2]
        send("ZP", k, zs_p.at[k], zr_p.at[k], dev(dzl=1))

    def p3(k):
        if k in PRE_DIRECT:
            got("D1", k, rd1.at[k, pl.ds(0, 2 * NY - 1)])
            v = total(rd1.at[k]) + encb_v[...]
        else:
            got("ZP", k, zr_p.at[k])
            v = zs_p[k] + zr_p[k] + encb_v[...]
        v2 = v * v
        t = jnp.tanh(A0 * (v * (1.0 + A1 * v2)))
        h = 0.5 * (1.0 + t)
        acts[piece(k, y), pl.ds(0, feats)] = (v * h).astype(BF)
        for o in FAR_FIRST:
            r = acts.at[piece(k, y), pl.ds(0, feats)]
            send("YA", k, r, r, dev(dy=o))
        gpr[k] = h + 0.5 * v * (1.0 - t * t) * (A0 * (1.0 + 3.0 * A1 * v2))

    def p4(k):
        got("YA", k, acts.at[pl.ds(0, 3 * rows), pl.ds(0, feats)])
        send("SA", k, acts.at[span(k), pl.ds(0, feats)], acts.at[span(k), pl.ds(feats, feats)], dev(dc=1))

    def p5(k):
        got("SA", k, acts.at[span(k), pl.ds(feats, feats)])

        if k == 0:
            pltpu.make_async_copy(w.at[pl.ds(0, feats)], w.at[pl.ds(0, feats)], lsem.at[2]).wait()
            got1("W", w.at[pl.ds(feats, feats)])

        a = acts[span(k)]
        s = span(k)
        for o in (2, 1, 3):
            rec[s, pl.ds(o * group, group)] = dot(a, w[:, pl.ds(o * group, group)], ((1,), (0,))).astype(BF)
            if o == 2:
                send("HP", k, rec.at[s, pl.ds(2 * group, hg)], hp.at[s], dev(dx=1))
                send("HM", k, rec.at[s, pl.ds(2 * group + hg, hg)], hm.at[s], dev(dx=3))
            elif o == 1:
                send("OP", k, rec.at[s, pl.ds(group + hg, hg)], op.at[s], dev(dx=1))
            else:
                send("OM", k, rec.at[s, pl.ds(3 * group, hg)], om.at[s], dev(dx=3))
        own[s] = dot(a, w[:, pl.ds(0, group)], ((1,), (0,)))

    def p6a(k):
        s = span(k)
        got("HP", k, hp.at[s])
        sp[s] = (hp[s].astype(F32) + rec[s, pl.ds(group, hg)].astype(F32)).astype(BF)
        send("AP", k, sp.at[s], ap.at[s], dev(dx=1))
        got("HM", k, hm.at[s])
        sm[s] = (hm[s].astype(F32) + rec[s, pl.ds(3 * group + hg, hg)].astype(F32)).astype(BF)
        send("AM", k, sm.at[s], am.at[s], dev(dx=3))

    def p6(k):
        s = span(k)
        got("OP", k, op.at[s])
        got("OM", k, om.at[s])
        got("AP", k, ap.at[s])
        got("AM", k, am.at[s])
        first = own[s, pl.ds(0, hg)] + ap[s].astype(F32) + om[s].astype(F32)
        second = own[s, pl.ds(hg, hg)] + am[s].astype(F32) + op[s].astype(F32)
        zown[s] = first[:, :blk]
        zsend[s, pl.ds(0, hg)] = first.astype(BF)
        zsend[s, pl.ds(hg, hg)] = second.astype(BF)
        for p in FAR_FIRST:
            send("ZR", k, zsend.at[s, pl.ds(p * blk, blk)], rz.at[k, p - 1], dev(dzh=p))

    def p7(k):
        s = span(k)
        got("ZR", k, rz.at[k])
        recon = zown[s] + rz[k, 0].astype(F32) + rz[k, 1].astype(F32) + rz[k, 2].astype(F32)

        if k == 0:
            c_tgt.wait()
            c_decb.wait()

        err = recon + decb_v[...] - tgt[s].astype(F32)
        eall[s, pl.ds(0, blk)] = err.astype(BF)
        for p in FAR_FIRST:
            send("ZA", k, eall.at[s, pl.ds(0, blk)], eall.at[s, pl.ds((NZ - p) * blk, blk)], dev(dzh=p))
        bsum[...] += fold(err)
        sq[...] += fold(err * err)

    def p8(k):
        s = span(k)
        got("ZA", k, eall.at[s, pl.ds(blk, 3 * blk)])
        send("XP", k, eall.at[s, pl.ds(0, group)], eall.at[s, pl.ds(3 * group, group)], dev(dx=1))
        send("XM", k, eall.at[s, pl.ds(0, group)], eall.at[s, pl.ds(group, group)], dev(dx=3))
        if k in X_DIRECT:
            send("X2", k, eall.at[s, pl.ds(0, group)], eall.at[s, pl.ds(2 * group, group)], dev(dx=2))

    def p8a(k):
        s = span(k)
        got("XP", k, eall.at[s, pl.ds(3 * group, group)])
        send("FP", k, eall.at[s, pl.ds(3 * group, hg)], eall.at[s, pl.ds(2 * group, hg)], dev(dx=1))
        got("XM", k, eall.at[s, pl.ds(group, group)])
        send("FM", k, eall.at[s, pl.ds(group + hg, hg)], eall.at[s, pl.ds(2 * group + hg, hg)], dev(dx=3))

    def p9(k):
        s = span(k)
        late = k == last_p9
        if k in X_DIRECT:
            got("XP", k, eall.at[s, pl.ds(3 * group, group)])
            got("XM", k, eall.at[s, pl.ds(group, group)])
        if late:
            for c in (pl.ds(0, 2 * group), pl.ds(3 * group, group)):
                b_send[s] += dot(eall[s, c], wt[c, pl.ds(feats, feats)], ((1,), (0,)))
                b_own[s] += dot(eall[s, c], wt[c, pl.ds(0, feats)], ((1,), (0,)))
        if k in X_DIRECT:
            got("X2", k, eall.at[s, pl.ds(2 * group, group)])
        else:
            got("FP", k, eall.at[s, pl.ds(2 * group, hg)])
            got("FM", k, eall.at[s, pl.ds(2 * group + hg, hg)])
        if late:
            c = pl.ds(2 * group, group)
            b_send[s] += dot(eall[s, c], wt[c, pl.ds(feats, feats)], ((1,), (0,)))
            send("SB", k, b_send.at[s], b_recv.at[s], dev(dc=1))
            b_own[s] += dot(eall[s, c], wt[c, pl.ds(0, feats)], ((1,), (0,)))
        else:
            e = eall[s]
            b_send[s] = dot(e, wt[:, pl.ds(feats, feats)], ((1,), (0,)))
            send("SB", k, b_send.at[s], b_recv.at[s], dev(dc=1))
            b_own[s] = dot(e, wt[:, pl.ds(0, feats)], ((1,), (0,)))

    def p10(k):
        s = span(k)
        got("SB", k, b_recv.at[s])
        by[s] = (b_own[s] + b_recv[s]).astype(BF)
        if k in BACK_DIRECT:
            everyone("D2", k, by, rd2.at[k])
            return
        for o in FAR_FIRST:
            send("YB", k, by.at[piece(k, (y + o) % NY)], ryb.at[k, o - 1], dev(dy=o))

    def p11(k):
        got("YB", k, ryb.at[k])
        me = piece(k, y)
        zs_b[k] = (
            b_own[me] + b_recv[me] + ryb[k, 0].astype(F32) + ryb[k, 1].astype(F32) + ryb[k, 2].astype(F32)
        )
        send("ZB", k, zs_b.at[k], zr_b.at[k], dev(dzl=1))

    def p12(k):
        if k in BACK_DIRECT:
            got("D2", k, rd2.at[k, pl.ds(0, 2 * NY - 1)])
            dpre = total(rd2.at[k]) * gpr[k]
        else:
            got("ZB", k, zr_b.at[k])
            dpre = (zs_b[k] + zr_b[k]) * gpr[k]
        r = dall.at[piece(k, y)]
        dall[piece(k, y)] = dpre.astype(BF)
        for o in FAR_FIRST:
            send("YD", k, r, r, dev(dy=o))
        pb[...] += fold(dpre)


    def p13(k):
        got("YD", k, dall.at[pl.ds(0, 3 * rows)])

    stages = dict(P1=p1, P2=p2, P3=p3, P4=p4, P5=p5, P6A=p6a, P6=p6, P7=p7, P8=p8, P8A=p8a, P9=p9, P10=p10, P11=p11, P12=p12)

    def grad(base, which):
        def body(n, _):
            at = pl.multiple_of(n * group, group)
            gd[pl.ds(base, feats), pl.ds(at, group)] = dot(
                acts[:, pl.ds(base, feats)], eall[:, pl.ds(at, group)], ((0,), (0,))
            ).astype(BF)
            for p in range(NZ):
                part = gd.at[pl.ds(base, feats), pl.ds(pl.multiple_of(at + p * blk, blk), blk)]
                where = gd_h.at[0, :, pl.ds(column(n, p, core), blk)]
                if which:
                    send1("GD", part, where, dev(dc=1))
                else:
                    pltpu.make_async_copy(part, where, lsem.at[4]).start()
            return 0

        lax.fori_loop(0, NX, body, 0)

    def bias():
        for o in range(1, NY):
            send1("GB", pb, rpb.at[o - 1], dev(dy=o))

    def l1():
        for o in range(1, NZ):
            send1("L1", sq, rl1.at[o - 1], dev(dzh=o))

    def l2():
        got1("L1", rl1)
        sl2[...] = sq[...] + rl1[0] + rl1[1] + rl1[2]
        for o in range(1, NX):
            send1("L2", sl2, rl2.at[o - 1], dev(dx=o))

    def l3():
        got1("L2", rl2)
        sl3[...] = sl2[...] + rl2[0] + rl2[1] + rl2[2]
        send1("L3", sl3, rl3, dev(dc=1))

    def l4():
        got1("L3", rl3)
        sl4[...] = sl3[...] + rl3[...]
        for o in range(1, NY):
            send1("L4", sl4, rl4.at[o - 1], dev(dy=o))

    def l5():
        got1("L4", rl4)
        sl5[...] = sl4[...] + rl4[0] + rl4[1] + rl4[2]
        send1("L5", sl5, rl5, dev(dzl=1))

    side = {"P7": (l1,), "P8": (l2,), "P9": (l3,), "P10": (l4,), "P12": (bias, l5)}
    left_of = [sum(c // 16 == i for c in SCHEDULE) for i in range(len(STAGES) + 1)]
    for at, code in enumerate(SCHEDULE):
        if at == 0:
            swap()
        stage, k = code // 16, code % 16
        if stage == len(STAGES):
            grad(feats * (1 - k), k == 0)
            continue
        name = STAGES[stage]
        stages[name](k)
        seen = left_of[4]
        left_of[stage] -= 1
        if name == "P5" and nch - NX - 1 < seen <= nch - 1:
            q = pl.ds((nch - 1 - seen) * group, group)
            wt[q, :] = w[:, q].T
        if left_of[stage] == 0:
            for step in side.get(name, ()):
                step()

    gdb_v[...] = jnp.sum(bsum[...], axis=0, keepdims=True)
    for k in range(nch):
        if k != last_p12:
            p13(k)

    def drain(kind, ref, only=None, skip=()):
        for k in range(nch) if only is None else only:
            if k not in skip:
                r = ref(k)
                pltpu.make_async_copy(r, r, ssem.at[ID[kind]]).wait()

    most = 2 * NY - 1
    drain("YR", lambda k: ry.at[k], skip=PRE_DIRECT)
    drain("ZP", lambda k: zr_p.at[k], skip=PRE_DIRECT)
    drain("D1", lambda k: rd1.at[k, pl.ds(0, most)], only=PRE_DIRECT)
    drain("YB", lambda k: ryb.at[k], skip=BACK_DIRECT)
    drain("ZB", lambda k: zr_b.at[k], skip=BACK_DIRECT)
    drain("D2", lambda k: rd2.at[k, pl.ds(0, most)], only=BACK_DIRECT)
    drain("FP", lambda k: hp.at[span(k)], skip=X_DIRECT)
    drain("FM", lambda k: hm.at[span(k)], skip=X_DIRECT)
    drain("X2", lambda k: eall.at[span(k), pl.ds(0, group)], only=X_DIRECT)
    q3 = 3 * tok // 4
    left = dict(
        YA=acts.at[pl.ds(0, q3), pl.ds(0, feats)], SA=acts.at[:, pl.ds(0, feats)], HP=hp, HM=hm, OP=op, OM=om, AP=ap, AM=am,
        ZR=rz, ZA=eall.at[:, pl.ds(0, 3 * blk)], XP=eall.at[:, pl.ds(0, group)], XM=eall.at[:, pl.ds(0, group)], SB=b_recv,
    )
    for name, ref in left.items():
        pltpu.make_async_copy(ref, ref, ssem.at[ID[name]]).wait()
    once = dict(W=w.at[pl.ds(0, feats)], L1=rl1, L2=rl2, L3=rl3, L4=rl4)
    for name, ref in once.items():
        pltpu.make_async_copy(ref, ref, oss.at[OID[name]]).wait()
    own_gd = gd.at[pl.ds(0, feats)]
    pltpu.make_async_copy(own_gd, own_gd, lsem.at[4]).wait()
    got1("L5", rl5)
    loss_s[0, 0] = jnp.sum(sl5[...] + rl5[...]) / (2.0 * tok * (2 * NY) * (2 * half))

    p13(last_p12)
    ge_v[...] = dot(src[...], dall[...], ((0,), (0,)))
    got1("GB", rpb)
    geb_v[...] = jnp.sum(pb[...] + rpb[0] + rpb[1] + rpb[2], axis=0, keepdims=True)
    got1("GD", own_gd)
    r = dall.at[pl.ds(0, q3)]
    pltpu.make_async_copy(r, r, ssem.at[ID["YD"]]).wait()
    for name, ref in dict(GB=rpb, L5=rl5, GD=own_gd).items():
        pltpu.make_async_copy(ref, ref, oss.at[OID[name]]).wait()


def place(a, b, c, d, ao, bo, co, do, sem):
    parts = [(b, bo), (d, do)]
    for i in range(4):
        r = pl.ds(i * (c.shape[1] // 4), c.shape[1] // 4)
        parts.append((c.at[:, r], co.at[:, r]))
    for i in range(2):
        r = pl.ds(i * (a.shape[0] // 2), a.shape[0] // 2)
        parts.append((a.at[r], ao.at[r]))
    copies = [pltpu.make_async_copy(i, o, sem.at[n]) for n, (i, o) in enumerate(parts)]
    for copy in copies:
        copy.start()
    for copy in copies:
        copy.wait()


def shards(source, enc_weight, enc_bias, dec_weight, dec_bias, target):
    tok, depth = source.shape
    feats = enc_weight.shape[1]
    width = dec_weight.shape[2]
    half = width // 2
    group = half // NX
    hg = group // 2
    blk = group // NZ
    nch = tok // CHUNK
    rows = CHUNK // NY
    V = pltpu.VMEM
    any_spec = pl.BlockSpec(memory_space=pl.ANY)
    hbm_spec = pl.BlockSpec(memory_space=pltpu.HBM)
    vmem_spec = pl.BlockSpec(memory_space=pltpu.VMEM)
    scratch = [
        V((tok, depth), BF), V((depth, feats), BF), V((tok, blk), BF), V((1, feats), F32), V((1, blk), F32), V((2 * feats, half), BF),
        V((tok, feats), F32), V((nch, 3, rows, feats), F32), V((nch, rows, feats), F32), V((nch, rows, feats), F32),
        V((nch, rows, feats), F32), V((tok, 2 * feats), BF), V((tok, half), BF), V((tok, group), F32),
        V((tok, hg), BF), V((tok, hg), BF), V((tok, hg), BF), V((tok, hg), BF), V((tok, hg), BF), V((tok, hg), BF),
        V((tok, hg), BF), V((tok, hg), BF), V((tok, group), BF), V((tok, blk), F32), V((nch, 3, CHUNK, blk), BF), V((tok, half), BF),
        V((tok, feats), F32), V((tok, feats), F32), V((tok, feats), F32), V((tok, feats), BF), V((nch, 3, rows, feats), BF),
        V((nch, rows, feats), F32), V((nch, rows, feats), F32), V((tok, feats), BF), V((2 * feats, half), BF),
        V((8, feats), F32), V((3, 8, feats), F32), V((8, blk), F32), V((3, 8, blk), F32), V((3, 8, blk), F32), V((8, blk), F32),
        V((3, 8, blk), F32), V((8, blk), F32), V((8, blk), F32), V((8, blk), F32), V((8, blk), F32), V((8, blk), F32), V((8, blk), F32),
        V((tok, feats), BF), V((nch, 2 * NY, rows, feats), BF), V((nch, 2 * NY, rows, feats), BF), V((half, 2 * feats), BF),
        pltpu.SemaphoreType.DMA((7,)), pltpu.SemaphoreType.DMA((len(KINDS),)), pltpu.SemaphoreType.DMA((len(KINDS), nch)),
        pltpu.SemaphoreType.DMA((len(ONCE),)), pltpu.SemaphoreType.DMA((len(ONCE),)),
    ]
    ge, geb, gd, gdb, loss = pl.pallas_call(
        kernel,
        out_shape=(
            jax.ShapeDtypeStruct((depth, feats), F32),
            jax.ShapeDtypeStruct((1, feats), F32),
            jax.ShapeDtypeStruct((1, feats, width), BF),
            jax.ShapeDtypeStruct((1, blk), F32),
            jax.ShapeDtypeStruct((1, 1), F32),
        ),
        in_specs=[any_spec] * 6,
        out_specs=(vmem_spec, vmem_spec, any_spec, vmem_spec, pl.BlockSpec(memory_space=pltpu.SMEM)),
        scratch_shapes=scratch,
        compiler_params=pltpu.CompilerParams(collective_id=0, has_side_effects=True, vmem_limit_bytes=45 << 20),
    )(*(pltpu.with_memory_space_constraint(v, pltpu.HBM) for v in (source, enc_weight, enc_bias.reshape(1, feats), dec_weight, dec_bias, target)))
    outs = (ge, geb, gd, gdb)
    ge, geb, gd, gdb = pl.pallas_call(
        place,
        out_shape=tuple(pltpu.HBM(v.shape, v.dtype) for v in outs),
        in_specs=[any_spec] * 4,
        out_specs=(any_spec,) * 4,
        scratch_shapes=[pltpu.SemaphoreType.DMA((8,))],
        compiler_params=pltpu.CompilerParams(vmem_limit_bytes=1 << 20),
    )(*(pltpu.with_memory_space_constraint(v, pltpu.VMEM) for v in outs))
    return ge, geb.reshape(feats), gd, gdb, loss.reshape(())


def solution(mesh):
    return jax.shard_map(
        shards,
        mesh=mesh,
        in_specs=(
            P(None, "layer"),
            P("layer", "feat"),
            P("feat"),
            P("layer", "feat", None),
            P("layer", None),
            P("layer", None, None),
        ),
        out_specs=(
            P("layer", "feat"),
            P("feat"),
            P("layer", "feat", None),
            P("layer", "feat"),
            P(),
        ),
        check_vma=False,
    )
```
